256 devices in a mesh: grp: 2 (over core), gx: 16 (over y, z_lo), gy: 8 (over z_hi, x).
Axes of the slice: x: 4, y: 4, z: 8 (z_hi: 2, z_lo: 4; z = z_hi * 4 + z_lo), core: 2. Of those that a mesh axis runs over, the one named last changes fastest.
Arguments:
- present_displacement: float32 [16, 512, 512], P('grp', ('gx', 'gy')), may hold values from -6 to 6
- prior_displacement: float32 [16, 512, 512], P('grp', ('gx', 'gy')), may hold values from -6 to 6
- fracture_state: float32 [16, 512, 512], P('grp', ('gx', 'gy')), may hold values from 0 to 0.6
- grid_material_region: int32 [16, 512, 512], P('grp', ('gx', 'gy')), may hold values from 0 to 5
- region_young_stiffness: float32 [6], replicated, may hold values from 0.3 to 1.5
- borehole_grid_position: int32 [64], replicated, may hold values from 0 to 4194303
- detonation_order: int32 [64], replicated, may hold values from 0 to 63, each once
- explosive_mass: float32 [64], replicated, may hold values from 2 to 8
- output_loss_sensitivity: float32 [16, 512, 512], P(('grp', 'gy'), 'gx'), may hold values from -6 to 6
- encoder_matrix: float32 [4, 32], replicated, may hold values from -3 to 3
- encoder_offset: float32 [32], replicated, may hold values from -3 to 3
- fourier_mode_kernel: float32 [2, 16, 32, 2, 32, 32], P(None, 'gx'), may hold values from -6 to 6
- local_mixing_matrix: float32 [2, 32, 32], replicated, may hold values from -1 to 1
- local_mixing_offset: float32 [2, 32], replicated, may hold values from -3 to 3
- decoder_matrix: float32 [32], replicated, may hold values from -1 to 1
Outputs:
- advanced_displacement: float32 [16, 512, 512], P('grp', ('gx', 'gy'))
- advanced_fracture_state: float32 [16, 512, 512], P('grp', ('gx', 'gy'))
- spec_grad: float32 [2, 16, 32, 2, 32, 32], P(None, 'gx')
- mix_grad: float32 [2, 32, 32], replicated
The draws below stay inside these ranges and needn't reach their ends.
Inputs may be any that keep to these rules, and one draw needn't show every extreme that they name: `borehole_grid_position`: flat cell indices z * 512 * 512 + x * 512 + y. `detonation_order`: each order 0 .. 63 once.
All inputs are finite; a program needn't handle non-finite values.
Results may differ from the reference program's by a relative error of at most 0.0003.
Values sent between devices are 32-bit elements; how exact they have to be, the bound alone decides.
No kernel may reach another device: no remote copies, remote signals or barrier semaphores. Data moves between devices by JAX's collectives and lax.ppermute only.
A program may use at most 64 MiB of HBM per device.

```python
import math
import jax
import jax.numpy as jnp
from jax import lax

NX = 512
NY = 512
MODES = 16
CHAN = 32
LAYERS = 2
FIELDS = 4
DRILLED_SHOTS = 64
NZONE = 6
NZ = 16


def set_ends(entries, key, smallest, largest):
    longest = entries.shape.index(max(entries.shape))
    spots = []
    for shift in (0, 1):
        where = [jax.random.randint(jax.random.fold_in(key, axis), (), 0, length) for axis, length in enumerate(entries.shape)]
        where[longest] = (where[longest] + shift) % entries.shape[longest]
        spots.append(tuple(where))
    return entries.at[spots[0]].set(smallest).at[spots[1]].set(largest)


def block_scale(own_key, shape, cuts, least, largest):
    def one(axis_at, shards_of):
        heights = jax.random.uniform(jax.random.fold_in(jax.random.fold_in(own_key, 6), axis_at), (shards_of,), jnp.float32, least / len(cuts), largest / len(cuts))
        return jnp.repeat(jnp.exp(heights), shape[axis_at] // shards_of).reshape((-1,) + (1,) * (len(shape) - axis_at - 1))

    gain = one(*cuts[0])
    for cut in cuts[1:]:
        gain = gain * one(*cut)
    return gain


def bell_draw(key, shape, deviation, most, cuts=(), kind=jnp.bfloat16):
    result = deviation * jax.random.normal(key, shape, jnp.float32)
    if cuts:
        result = result * block_scale(key, shape, cuts, -0.22, 0.18)
    return jnp.clip(result, -most, most).astype(kind)


def setup_inputs(seed: int = 0) -> dict:
    splits = jax.random.split(jax.random.key(seed), 16)
    present_displacement = bell_draw(splits[0], (NZ, NX, NY), 1.0, 6.0, ((0, 2), (1, 128)), jnp.float32)
    prior_displacement = bell_draw(splits[1], (NZ, NX, NY), 1.0, 6.0, ((0, 2), (1, 128)), jnp.float32)
    fracture_state = jnp.clip(0.6 * jax.random.uniform(splits[2], (NZ, NX, NY), jnp.float32) ** block_scale(splits[2], (NZ, NX, NY), ((0, 2), (1, 128)), -0.2, 0.2), 0.0, 0.6)
    grid_material_region = set_ends(jax.random.randint(splits[3], (NZ, NX, NY), 0, NZONE), jax.random.fold_in(splits[3], 1), 0, NZONE - 1).astype(jnp.int32)
    region_young_stiffness = jnp.clip(jnp.exp(jax.random.uniform(splits[4], (NZONE,), jnp.float32, math.log(0.3), math.log(1.5))), 0.3, 1.5)
    borehole_grid_position = set_ends(jax.random.randint(splits[5], (DRILLED_SHOTS,), 0, NZ * NX * NY), jax.random.fold_in(splits[5], 1), 0, (NZ * NX * NY) - 1).astype(jnp.int32)
    detonation_order = jax.random.permutation(splits[6], DRILLED_SHOTS).astype(jnp.int32)
    explosive_mass = jnp.clip(jnp.exp(jax.random.uniform(splits[7], (DRILLED_SHOTS,), jnp.float32, math.log(2.0), math.log(8.0))), 2.0, 8.0)
    output_loss_sensitivity = bell_draw(splits[8], (NZ, NX, NY), 1.0, 6.0, ((0, 16), (1, 16)), jnp.float32)
    encoder_matrix = bell_draw(splits[9], (FIELDS, CHAN), FIELDS ** -0.5, 3.0, (), jnp.float32)
    encoder_offset = bell_draw(splits[10], (CHAN,), 0.5, 3.0, (), jnp.float32)
    fourier_mode_kernel = bell_draw(splits[11], (LAYERS, MODES, 2 * MODES, 2, CHAN, CHAN), ((NX * NY / (8 * MODES * MODES * CHAN)) ** 0.5), 6.0, ((1, 16),), jnp.float32)
    local_mixing_matrix = bell_draw(splits[12], (LAYERS, CHAN, CHAN), CHAN ** -0.5, 1.0, (), jnp.float32)
    local_mixing_offset = bell_draw(splits[13], (LAYERS, CHAN), 0.5, 3.0, (), jnp.float32)
    decoder_matrix = bell_draw(splits[14], (CHAN,), CHAN ** -0.5, 1.0, (), jnp.float32)
    return dict(present_displacement=present_displacement, prior_displacement=prior_displacement, fracture_state=fracture_state, grid_material_region=grid_material_region, region_young_stiffness=region_young_stiffness, borehole_grid_position=borehole_grid_position, detonation_order=detonation_order, explosive_mass=explosive_mass, output_loss_sensitivity=output_loss_sensitivity, encoder_matrix=encoder_matrix, encoder_offset=encoder_offset, fourier_mode_kernel=fourier_mode_kernel, local_mixing_matrix=local_mixing_matrix, local_mixing_offset=local_mixing_offset, decoder_matrix=decoder_matrix)


highest = lax.Precision.HIGHEST
courant = 0.08
damage_rate = 0.5
strain_limit = 1.0
borehole_attenuation = 0.95

def fracture_time_advance(present_displacement, prior_displacement, fracture_state, grid_material_region, region_young_stiffness, borehole_grid_position, detonation_order, explosive_mass):
    padded = jnp.pad(present_displacement, 1)
    laplace = padded[2:, 1:-1, 1:-1] + padded[:-2, 1:-1, 1:-1] + padded[1:-1, 2:, 1:-1] + padded[1:-1, :-2, 1:-1] + padded[1:-1, 1:-1, 2:] + padded[1:-1, 1:-1, :-2] - 6.0 * present_displacement
    strain_z = 0.5 * (padded[2:, 1:-1, 1:-1] - padded[:-2, 1:-1, 1:-1])
    strain_x = 0.5 * (padded[1:-1, 2:, 1:-1] - padded[1:-1, :-2, 1:-1])
    strain_y = 0.5 * (padded[1:-1, 1:-1, 2:] - padded[1:-1, 1:-1, :-2])
    modulus = jnp.zeros(present_displacement.shape, jnp.float32)
    for zone_index in range(region_young_stiffness.shape[0]):
        modulus = modulus + jnp.where(grid_material_region == zone_index, region_young_stiffness[zone_index], 0.0)
    stiffness = modulus * (1.0 - fracture_state)
    displacement_magnitude = explosive_mass * jnp.power(borehole_attenuation, detonation_order.astype(jnp.float32))
    source = jnp.zeros(NZ * NX * NY, jnp.float32).at[borehole_grid_position].add(displacement_magnitude).reshape(present_displacement.shape)
    advanced_displacement = 2.0 * present_displacement - prior_displacement + courant * stiffness * laplace + source
    strain_sq = strain_x * strain_x + strain_y * strain_y + strain_z * strain_z
    advanced_fracture_state = fracture_state + (1.0 - fracture_state) * jnp.tanh(damage_rate * jnp.maximum(strain_sq - strain_limit, 0.0))
    latent_width = jnp.stack([advanced_displacement, advanced_fracture_state, stiffness * strain_x, stiffness * strain_y], 0)
    return (advanced_displacement, advanced_fracture_state, latent_width)

def forward_modes(field_in):
    along_y = jnp.fft.rfft(field_in, axis=3)[..., :MODES] / NY
    along_x = jnp.fft.fft(along_y, axis=2) / NX
    return jnp.concatenate([along_x[:, :, :MODES], along_x[:, :, NX - MODES:]], 2)

def analysis(field_in, double):
    along_y = jnp.fft.rfft(field_in, axis=3)[..., :MODES] * double
    along_x = jnp.fft.fft(along_y, axis=2)
    return jnp.concatenate([along_x[:, :, :MODES], along_x[:, :, NX - MODES:]], 2)

def synthesis(modes_in):
    chan_count, plane_count = (modes_in.shape[0], modes_in.shape[1])
    middle = jnp.zeros((chan_count, plane_count, NX - 2 * MODES, MODES), modes_in.dtype)
    spectrum = jnp.concatenate([modes_in[:, :, :MODES], middle, modes_in[:, :, MODES:]], 2)
    rows_x = jnp.fft.ifft(spectrum, axis=2) * NX
    upper = jnp.zeros((chan_count, plane_count, NX, NY // 2 + 1 - MODES), rows_x.dtype)
    return jnp.fft.irfft(jnp.concatenate([rows_x, upper], 3), n=NY, axis=3) * NY

def reference(present_displacement, prior_displacement, fracture_state, grid_material_region, region_young_stiffness, borehole_grid_position, detonation_order, explosive_mass, output_loss_sensitivity, encoder_matrix, encoder_offset, fourier_mode_kernel, local_mixing_matrix, local_mixing_offset, decoder_matrix):
    advanced_displacement, advanced_fracture_state, latent_width = fracture_time_advance(present_displacement, prior_displacement, fracture_state, grid_material_region, region_young_stiffness, borehole_grid_position, detonation_order, explosive_mass)
    double = jnp.where(jnp.arange(MODES, dtype=jnp.int32) == 0, 1.0, 2.0).astype(jnp.float32)
    weight_c = fourier_mode_kernel[:, :, :, 0] + 1j * fourier_mode_kernel[:, :, :, 1]

    def plane_step(totals, inputs):
        spec_total, mix_total = totals
        feature_plane, cot_plane = inputs
        activation = jnp.einsum('fxy,fc->cxy', feature_plane, encoder_matrix, precision=highest)[:, None]
        activation = activation + encoder_offset[:, None, None, None]
        kept = []
        for layer_index in range(LAYERS):
            modes_in = forward_modes(activation)
            mixed = jnp.einsum('izkm,mkio->ozkm', modes_in, weight_c[layer_index], precision=highest)
            pre_act = synthesis(mixed) + jnp.einsum('izxy,io->ozxy', activation, local_mixing_matrix[layer_index], precision=highest) + local_mixing_offset[layer_index][:, None, None, None]
            kept.append((activation, pre_act, modes_in))
            activation = jax.nn.gelu(pre_act)
        gradient = decoder_matrix[:, None, None, None] * cot_plane[None, None]
        spec_list = []
        mix_list = []
        for layer_index in reversed(range(LAYERS)):
            act_in, pre_act, modes_in = kept[layer_index]
            _, pullback = jax.vjp(jax.nn.gelu, pre_act)
            grad_act = pullback(gradient)[0]
            grad_modes = analysis(grad_act, double)
            spec_c = jnp.einsum('izkm,ozkm->mkio', jnp.conj(modes_in), grad_modes, precision=highest)
            spec_list.append(jnp.stack([jnp.real(spec_c), jnp.imag(spec_c)], 2))
            mix_list.append(jnp.einsum('izxy,ozxy->io', act_in, grad_act, precision=highest))
            if layer_index > 0:
                back = jnp.einsum('ozkm,mkio->izkm', grad_modes, jnp.conj(weight_c[layer_index]), precision=highest)
                gradient = synthesis(back / double) / (NX * NY) + jnp.einsum('ozxy,io->izxy', grad_act, local_mixing_matrix[layer_index], precision=highest)
        spec_total = spec_total + jnp.stack(spec_list[::-1], 0)
        mix_total = mix_total + jnp.stack(mix_list[::-1], 0)
        return ((spec_total, mix_total), None)
    start_totals = (jnp.zeros((LAYERS, MODES, 2 * MODES, 2, CHAN, CHAN), jnp.float32), jnp.zeros((LAYERS, CHAN, CHAN), jnp.float32))
    (spec_grad, mix_total), _ = lax.scan(plane_step, start_totals, (jnp.transpose(latent_width, (1, 0, 2, 3)), output_loss_sensitivity))
    return (advanced_displacement, advanced_fracture_state, spec_grad, mix_total / math.sqrt(NX * NY))
```

```python
import math

import jax
import jax.numpy as jnp
from jax import lax
from jax.sharding import PartitionSpec as P

NX = 512
NY = 512
MODES = 16
LAYERS = 2


highest = lax.Precision.HIGHEST
split = lax.Precision.HIGH
courant = 0.08
damage_rate = 0.5
strain_limit = 1.0
borehole_attenuation = 0.95


def extended(cells, sides, width):
    for axis, dim in sides:
        count = lax.axis_size(axis)
        ends = count - 1
        head = lax.slice_in_dim(cells, 0, width, axis=dim)
        tail = lax.slice_in_dim(cells, cells.shape[dim] - width, cells.shape[dim], axis=dim)
        cells = jnp.concatenate(
            [
                lax.ppermute(tail, axis, [(i, (i + 1) % count) for i in range(ends)]),
                cells,
                lax.ppermute(head, axis, [((i + 1) % count, i) for i in range(ends)]),
            ],
            axis=dim,
        )
    return cells


def build_tables(size_x, size_y, modes):
    wave_y = jnp.arange(modes, dtype=jnp.int32)
    cells_y = jnp.arange(size_y, dtype=jnp.int32)
    angle_y = (
        2.0 * jnp.pi / size_y * (cells_y[:, None] * wave_y[None, :] % size_y).astype(jnp.float32)
    )
    cos_y = jnp.cos(angle_y)
    sin_y = jnp.sin(angle_y)
    double = jnp.where(wave_y == 0, 1.0, 2.0).astype(jnp.float32)
    forward_y = jnp.stack([cos_y, -sin_y], 2).reshape(size_y, 2 * modes) / size_y
    inverse_y = jnp.stack([cos_y * double, -sin_y * double], 2).reshape(size_y, 2 * modes).T
    wave_x = jnp.concatenate(
        [jnp.arange(modes, dtype=jnp.int32), size_x - modes + jnp.arange(modes, dtype=jnp.int32)]
    )
    cells_x = jnp.arange(size_x, dtype=jnp.int32)
    angle_x = (
        2.0 * jnp.pi / size_x * (cells_x[:, None] * wave_x[None, :] % size_x).astype(jnp.float32)
    )
    return (forward_y, inverse_y, jnp.cos(angle_x), jnp.sin(angle_x))


def sum_to_owners(rows, axis):
    count = lax.axis_size(axis)
    landed = lax.all_to_all(rows, axis, split_axis=0, concat_axis=0, tiled=True)
    return landed.reshape((count, rows.shape[0] // count) + rows.shape[1:]).sum(0)


def gather_blocks(block, axis):
    count = lax.axis_size(axis)
    copies = jnp.broadcast_to(block[None], (count,) + block.shape)
    return lax.all_to_all(copies, axis, split_axis=0, concat_axis=0, tiled=True)


def to_spectrum(field_in, table_y, cos_x, sin_x):
    channels, planes, local_x, length_y = field_in.shape
    kx_count = cos_x.shape[1]
    offset = lax.axis_index("gx") * local_x
    cos_local = lax.dynamic_slice_in_dim(cos_x, offset, local_x, 0)
    sin_local = lax.dynamic_slice_in_dim(sin_x, offset, local_x, 0)
    row_count = table_y.shape[1] // lax.axis_size("gx") * lax.axis_size("gx")
    transformed = jnp.einsum("czxy,yk->kczx", field_in, table_y, precision=highest)
    paired = transformed.reshape(row_count // 2, 2, channels, planes, local_x)
    real_in = paired[:, 0]
    imag_in = paired[:, 1]
    real_out = jnp.einsum("mczx,xk->mczk", real_in, cos_local, precision=highest) + jnp.einsum(
        "mczx,xk->mczk", imag_in, sin_local, precision=highest
    )
    imag_out = jnp.einsum("mczx,xk->mczk", imag_in, cos_local, precision=highest) - jnp.einsum(
        "mczx,xk->mczk", real_in, sin_local, precision=highest
    )
    partial = jnp.stack([real_out, imag_out], 1).reshape(row_count, channels, planes, kx_count)
    kept_rows = sum_to_owners(partial, "gx")
    paired = kept_rows.reshape(-1, 2, channels, planes, kx_count)
    real_out = jnp.transpose(paired[:, 0], (1, 2, 0, 3))
    imag_out = jnp.transpose(paired[:, 1], (1, 2, 0, 3))
    return (real_out, imag_out)


def from_spectrum(real_in, imag_in, cos_x, sin_x, table_inv):
    channels, planes, mode_count, kx_count = real_in.shape
    local_x = cos_x.shape[0] // lax.axis_size("gx")
    offset = lax.axis_index("gx") * local_x
    cos_local = lax.dynamic_slice_in_dim(cos_x, offset, local_x, 0)
    sin_local = lax.dynamic_slice_in_dim(sin_x, offset, local_x, 0)
    pieces = gather_blocks(jnp.stack([real_in, imag_in], 0), "gx")
    piece_real = jnp.moveaxis(pieces[:, 0], 0, 2).reshape(channels, planes, -1, kx_count)
    piece_imag = jnp.moveaxis(pieces[:, 1], 0, 2).reshape(channels, planes, -1, kx_count)
    piece_rows = piece_real.shape[2]
    real_x = jnp.einsum("czmk,xk->czmx", piece_real, cos_local, precision=highest) - jnp.einsum(
        "czmk,xk->czmx", piece_imag, sin_local, precision=highest
    )
    imag_x = jnp.einsum("czmk,xk->czmx", piece_imag, cos_local, precision=highest) + jnp.einsum(
        "czmk,xk->czmx", piece_real, sin_local, precision=highest
    )
    stacked = jnp.stack([real_x, imag_x], 3).reshape(channels, planes, 2 * piece_rows, local_x)
    return jnp.einsum("czkx,ky->czxy", stacked, table_inv, precision=highest)


def apply_modes(real_in, imag_in, weight_real, weight_imag):
    real_out = jnp.einsum("izmk,mkio->ozmk", real_in, weight_real, precision=split) - jnp.einsum(
        "izmk,mkio->ozmk", imag_in, weight_imag, precision=split
    )
    imag_out = jnp.einsum("izmk,mkio->ozmk", real_in, weight_imag, precision=split) + jnp.einsum(
        "izmk,mkio->ozmk", imag_in, weight_real, precision=split
    )
    return (real_out, imag_out)


def apply_adjoint(grad_real, grad_imag, weight_real, weight_imag):
    real_out = jnp.einsum(
        "ozmk,mkio->izmk", grad_real, weight_real, precision=split
    ) + jnp.einsum("ozmk,mkio->izmk", grad_imag, weight_imag, precision=split)
    imag_out = jnp.einsum(
        "ozmk,mkio->izmk", grad_imag, weight_real, precision=split
    ) - jnp.einsum("ozmk,mkio->izmk", grad_real, weight_imag, precision=split)
    return (real_out, imag_out)


def weight_terms(modes_real, modes_imag, grad_real, grad_imag):
    real_part = jnp.einsum(
        "izmk,ozmk->mkio", modes_real, grad_real, precision=split
    ) + jnp.einsum("izmk,ozmk->mkio", modes_imag, grad_imag, precision=split)
    imag_part = jnp.einsum(
        "izmk,ozmk->mkio", modes_real, grad_imag, precision=split
    ) - jnp.einsum("izmk,ozmk->mkio", modes_imag, grad_real, precision=split)
    return jnp.stack([real_part, imag_part], 2)


def shards(
    present_displacement,
    prior_displacement,
    fracture_state,
    grid_material_region,
    region_young_stiffness,
    borehole_grid_position,
    detonation_order,
    explosive_mass,
    output_loss_sensitivity,
    encoder_matrix,
    encoder_offset,
    fourier_mode_kernel,
    local_mixing_matrix,
    local_mixing_offset,
    decoder_matrix,
):
    depth_z, local_x, local_y = present_displacement.shape
    framed = extended(present_displacement, (("grp", 0), (("gx", "gy"), 1)), 1)
    padded = jnp.pad(framed, ((0, 0), (0, 0), (1, 1)))
    laplace = (
        padded[2:, 1:-1, 1:-1]
        + padded[:-2, 1:-1, 1:-1]
        + padded[1:-1, 2:, 1:-1]
        + padded[1:-1, :-2, 1:-1]
        + padded[1:-1, 1:-1, 2:]
        + padded[1:-1, 1:-1, :-2]
        - 6.0 * present_displacement
    )
    strain_z = 0.5 * (padded[2:, 1:-1, 1:-1] - padded[:-2, 1:-1, 1:-1])
    strain_x = 0.5 * (padded[1:-1, 2:, 1:-1] - padded[1:-1, :-2, 1:-1])
    strain_y = 0.5 * (padded[1:-1, 1:-1, 2:] - padded[1:-1, 1:-1, :-2])
    modulus = jnp.zeros(present_displacement.shape, jnp.float32)
    for zone_index in range(region_young_stiffness.shape[0]):
        modulus = modulus + jnp.where(
            grid_material_region == zone_index, region_young_stiffness[zone_index], 0.0
        )
    stiffness = modulus * (1.0 - fracture_state)
    displacement_magnitude = explosive_mass * jnp.power(
        borehole_attenuation, detonation_order.astype(jnp.float32)
    )
    plane_cells = NX * NY
    hole_z = borehole_grid_position // plane_cells
    remain = borehole_grid_position % plane_cells
    offset_z = hole_z - lax.axis_index("grp") * depth_z
    offset_x = remain // NY - lax.axis_index(("gx", "gy")) * local_x
    offset_y = remain % NY
    inside = (offset_z >= 0) & (offset_z < depth_z) & (offset_x >= 0) & (offset_x < local_x)
    brick_cells = depth_z * local_x * local_y
    flat_index = jnp.where(
        inside, (offset_z * local_x + offset_x) * local_y + offset_y, brick_cells
    )
    source = (
        jnp.zeros(brick_cells, jnp.float32)
        .at[flat_index]
        .add(displacement_magnitude, mode="drop")
        .reshape(present_displacement.shape)
    )
    advanced_displacement = (
        2.0 * present_displacement - prior_displacement + courant * stiffness * laplace + source
    )
    strain_sq = strain_x * strain_x + strain_y * strain_y + strain_z * strain_z
    advanced_fracture_state = fracture_state + (1.0 - fracture_state) * jnp.tanh(
        damage_rate * jnp.maximum(strain_sq - strain_limit, 0.0)
    )
    latent_width = jnp.stack(
        [
            advanced_displacement,
            advanced_fracture_state,
            stiffness * strain_x,
            stiffness * strain_y,
        ],
        0,
    )
    relaid = lax.all_to_all(latent_width, "gy", split_axis=1, concat_axis=2, tiled=True)
    forward_y, inverse_y, cos_x, sin_x = build_tables(NX, NY, MODES)
    cos_scaled = cos_x / NX
    sin_scaled = sin_x / NX
    activation = jnp.einsum("fzxy,fc->czxy", relaid, encoder_matrix, precision=split)
    activation = activation + encoder_offset[:, None, None, None]
    kept = []
    for layer_index in range(LAYERS):
        modes_real, modes_imag = to_spectrum(activation, forward_y, cos_scaled, sin_scaled)
        mixed_real, mixed_imag = apply_modes(
            modes_real,
            modes_imag,
            fourier_mode_kernel[layer_index, :, :, 0],
            fourier_mode_kernel[layer_index, :, :, 1],
        )
        pre_act = (
            from_spectrum(mixed_real, mixed_imag, cos_x, sin_x, inverse_y)
            + jnp.einsum(
                "izxy,io->ozxy", activation, local_mixing_matrix[layer_index], precision=split
            )
            + local_mixing_offset[layer_index][:, None, None, None]
        )
        kept.append((activation, pre_act, modes_real, modes_imag))
        activation = jax.nn.gelu(pre_act)
    gradient = decoder_matrix[:, None, None, None] * output_loss_sensitivity[None]
    spec_list = []
    mix_list = []
    for layer_index in reversed(range(LAYERS)):
        act_in, pre_act, modes_real, modes_imag = kept[layer_index]
        _, pullback = jax.vjp(jax.nn.gelu, pre_act)
        grad_act = pullback(gradient)[0]
        grad_real, grad_imag = to_spectrum(grad_act, inverse_y.T, cos_x, sin_x)
        weight_real = fourier_mode_kernel[layer_index, :, :, 0]
        weight_imag = fourier_mode_kernel[layer_index, :, :, 1]
        spec_list.append((modes_real, modes_imag, grad_real, grad_imag))
        mix_list.append(jnp.einsum("izxy,ozxy->io", act_in, grad_act, precision=split))
        if layer_index > 0:
            adj_real, adj_imag = apply_adjoint(grad_real, grad_imag, weight_real, weight_imag)
            gradient = from_spectrum(
                adj_real, adj_imag, cos_scaled, sin_scaled, forward_y.T
            ) + jnp.einsum(
                "ozxy,io->izxy", grad_act, local_mixing_matrix[layer_index], precision=split
            )
    spectra = jnp.stack([jnp.stack(part, 0) for part in spec_list[::-1]], 0)
    mix_parts = jnp.stack(mix_list[::-1], 0)
    mix_sum = gather_blocks(mix_parts, "gx").sum(0)
    message = jnp.concatenate([spectra.reshape(-1), mix_sum.reshape(-1)])
    landed = gather_blocks(message, ("grp", "gy"))
    planes_all = landed[:, : spectra.size].reshape((-1,) + spectra.shape)
    mix_total = landed[:, spectra.size :].sum(0).reshape(mix_parts.shape)
    spec_grad = []
    for layer_index in range(LAYERS):
        parts = [jnp.moveaxis(planes_all[:, layer_index, k, :, 0], 0, 1) for k in range(4)]
        spec_grad.append(weight_terms(*parts))
    spec_grad = jnp.stack(spec_grad, 0)
    return (
        advanced_displacement,
        advanced_fracture_state,
        spec_grad,
        mix_total / math.sqrt(NX * NY),
    )


def solution(mesh):
    return jax.shard_map(
        shards,
        mesh=mesh,
        in_specs=(
            P("grp", ("gx", "gy"), None),
            P("grp", ("gx", "gy"), None),
            P("grp", ("gx", "gy"), None),
            P("grp", ("gx", "gy"), None),
            P(),
            P(),
            P(),
            P(),
            P(("grp", "gy"), "gx", None),
            P(),
            P(),
            P(None, "gx", None, None, None, None),
            P(),
            P(),
            P(),
        ),
        out_specs=(
            P("grp", ("gx", "gy"), None),
            P("grp", ("gx", "gy"), None),
            P(None, "gx", None, None, None, None),
            P(),
        ),
        check_vma=False,
    )
```

```python
import math

import jax
import jax.numpy as jnp
import ml_dtypes
import numpy as np
from jax import lax
from jax.experimental import pallas as pl
from jax.experimental.pallas import tpu as pltpu
from jax.sharding import PartitionSpec as P

NX = 512
NY = 512
MODES = 16
CHAN = 32
FIELDS = 4
LAYERS = 2
GROUPS = 4
PER_GROUP = CHAN // GROUPS
ROWS = 32
KX = 2 * MODES
CELLS = NX * NY

highest = lax.Precision.HIGHEST
split = lax.Precision.HIGH
courant = 0.08
damage_rate = 0.5
strain_limit = 1.0
borehole_attenuation = 0.95
F32 = jnp.float32
BF16 = jnp.bfloat16
NN = (((1,), (0,)), ((), ()))
NT = (((1,), (1,)), ((), ()))
TN = (((0,), (0,)), ((), ()))
GELU_A = math.sqrt(2.0 / math.pi)
GELU_B = 0.044715
VMEM_LIMIT = 60 * 1024 * 1024


def parts_of(table, count):
    parts = []
    for _ in range(count):
        part = table.astype(ml_dtypes.bfloat16)
        parts.append(part)
        table = table - part.astype(np.float64)
    return parts


def wave_tables():
    ky = np.arange(MODES)
    angle_y = 2.0 * np.pi / NY * (ky[:, None] * np.arange(NY)[None, :] % NY)
    along_y = np.concatenate([np.cos(angle_y), -np.sin(angle_y)], 0)
    kx = np.concatenate([np.arange(MODES), NX - MODES + np.arange(MODES)])
    angle_x = 2.0 * np.pi / NX * (np.arange(NX)[:, None] * kx[None, :] % NX)
    y1, y2, y3 = parts_of(along_y, 3)
    forward_y = np.concatenate([y1, y2, y3], 0)
    inverse_y = np.concatenate([y1, y1, y2], 0)
    c1, c2 = parts_of(np.cos(angle_x), 2)
    s1, s2 = parts_of(np.sin(angle_x), 2)
    return forward_y, inverse_y, np.stack([c1, s1, c2, s2], 0)


def block_tables(along_x):
    local = lax.dynamic_slice_in_dim(along_x, lax.axis_index("gx") * ROWS, ROWS, 1)
    eye = jnp.eye(PER_GROUP, dtype=BF16)
    wide = eye[:, None, None, :, None] * jnp.transpose(local, (1, 0, 2))[None, :, :, None, :]
    return wide.reshape(PER_GROUP * ROWS, 4 * PER_GROUP * KX)


def halves(value):
    high = value.astype(BF16)
    return high, (value - high.astype(F32)).astype(BF16)


def dot(left, right, dims):
    return lax.dot_general(left, right, dims, preferred_element_type=F32)


def along_y(cells, forward_y):
    high, low = halves(cells)
    first = dot(forward_y[...], high, NT)
    second = dot(forward_y[: 4 * MODES, :], low, NT)
    return first[: 2 * MODES] + (
        first[2 * MODES : 4 * MODES]
        + first[4 * MODES :]
        + second[: 2 * MODES]
        + second[2 * MODES :]
    )


def along_x(pieces, blocks, dims, width):
    count = len(pieces)
    rows = 2 * MODES * count
    stacked = jnp.concatenate(halves(jnp.concatenate(pieces, 0)), 0)
    span = PER_GROUP * KX
    table = [blocks[:width, k * span : k * span + width] for k in range(4)]
    cos_1, sin_1 = [dot(stacked, part, dims) for part in table[:2]]
    cos_2, sin_2 = [dot(stacked[:rows], part, dims) for part in table[2:]]
    cos = cos_1[:rows] + (cos_1[rows:] + cos_2)
    sin = sin_1[:rows] + (sin_1[rows:] + sin_2)
    cut = [slice(2 * MODES * k, 2 * MODES * (k + 1)) for k in range(count)]
    return [(cos[at], sin[at]) for at in cut]


def forward_x(pieces, blocks, width):
    return [
        (cos[:MODES] + sin[MODES:], cos[MODES:] - sin[:MODES])
        for cos, sin in along_x(pieces, blocks, NN, width)
    ]


def inverse_x(modes, scaled, blocks, held):
    pieces = []
    for g in range(GROUPS):
        real = jnp.concatenate([modes[:, 2 * g, :], modes[:, 2 * g + 1, :]], 1)
        imag = jnp.concatenate([modes[:, 8 + 2 * g, :], modes[:, 9 + 2 * g, :]], 1)
        pieces.append(jnp.concatenate([scaled(real), scaled(imag)], 0))
    for g, (cos, sin) in enumerate(along_x(pieces, blocks, NT, PER_GROUP * ROWS)):
        rows = jnp.concatenate([cos[:MODES] - sin[MODES:], cos[MODES:] + sin[:MODES]], 0)
        high, low = halves(rows)
        held[g] = jnp.concatenate([high, low, high], 0)


def write_modes(sums, blocks, out):
    pieces = [sums[g] for g in range(GROUPS)]
    for g, (real, imag) in enumerate(forward_x(pieces, blocks, PER_GROUP * ROWS)):
        out[:, 2 * g, :] = real[:, :128]
        out[:, 2 * g + 1, :] = real[:, 128:]
        out[:, 8 + 2 * g, :] = imag[:, :128]
        out[:, 9 + 2 * g, :] = imag[:, 128:]


def doubled(value):
    row = lax.broadcasted_iota(jnp.int32, value.shape, 0)
    return jnp.where(row == 0, value, 2.0 * value)


def gelu_terms(value):
    square = value * value
    bend = jnp.tanh(GELU_A * value * (1.0 + GELU_B * square))
    half = 0.5 * (1.0 + bend)
    slope = half + value * (0.5 * (1.0 - bend * bend)) * (GELU_A * (1.0 + 3.0 * GELU_B * square))
    return value * half, slope


def before_kernel(place, stiff, position, charge, now, prior, fracture, region, base, stiffness):
    zones = region[...]
    modulus = jnp.zeros(zones.shape, F32)
    for k in range(stiff.shape[0]):
        modulus = jnp.where(zones == k, stiff[k], modulus)
    stiffness[...] = modulus * (1.0 - fracture[...])
    depth, rows, _ = now.shape
    cell = (
        (place[0] * depth + lax.broadcasted_iota(jnp.int32, now.shape, 0)) * CELLS
        + (place[1] * rows + lax.broadcasted_iota(jnp.int32, now.shape, 1)) * NY
        + lax.broadcasted_iota(jnp.int32, now.shape, 2)
    )
    source = jnp.zeros(now.shape, F32)
    for h in range(position.shape[0]):
        source = source + jnp.where(cell == position[h], charge[h], 0.0)
    base[...] = 2.0 * now[...] - prior[...] + source


def solver_kernel(place, now, over, above, below, base, stiffness, fracture, ahead, damage, fields, wide):
    depth, rows, _ = now.shape
    wide[...] = jnp.zeros(wide.shape, F32)
    wide[:, 1:2, :] = above[...]
    wide[:, 2 : 2 + rows, :] = now[...]
    wide[:, 2 + rows : 3 + rows, :] = below[...]
    upper = place[0] == 1
    lane = lax.broadcasted_iota(jnp.int32, (rows, NY), 1)
    for z in range(depth):
        here = now[z]
        other = over[0]
        before_z = now[z - 1] if z > 0 else jnp.where(upper, other, 0.0)
        after_z = now[z + 1] if z < depth - 1 else jnp.where(upper, 0.0, other)
        before_x = wide[z, 1 : 1 + rows, :]
        after_x = wide[z, 3 : 3 + rows, :]
        before_y = jnp.where(lane == 0, 0.0, pltpu.roll(here, 1, 1))
        after_y = jnp.where(lane == NY - 1, 0.0, pltpu.roll(here, NY - 1, 1))
        laplace = after_z + before_z + after_x + before_x + after_y + before_y - 6.0 * here
        strain_z = 0.5 * (after_z - before_z)
        strain_x = 0.5 * (after_x - before_x)
        strain_y = 0.5 * (after_y - before_y)
        stiff = stiffness[z]
        moved = base[z] + courant * stiff * laplace
        square = strain_x * strain_x + strain_y * strain_y + strain_z * strain_z
        broken = fracture[z]
        grown = broken + (1.0 - broken) * jnp.tanh(
            damage_rate * jnp.maximum(square - strain_limit, 0.0)
        )
        ahead[z] = moved
        damage[z] = grown
        fields[z, 0] = moved
        fields[z, 1] = grown
        fields[z, 2] = stiff * strain_x
        fields[z, 3] = stiff * strain_y


def field_kernel(landed, forward_y, blocks, fields, out):
    blocks_in, _, rows, _ = landed.shape
    for k in range(blocks_in):
        for f in range(FIELDS):
            fields[f, k * rows : (k + 1) * rows, :] = landed[k, f]
    sums = along_y(fields[...].reshape(FIELDS * ROWS, NY), forward_y)
    ((real, imag),) = forward_x([sums], blocks, FIELDS * ROWS)
    for k in range(out.shape[0]):
        out[k, :MODES, :] = real * (1.0 / CELLS)
        out[k, MODES:, :] = imag * (1.0 / CELLS)


def lift_kernel(landed, lifted, spread, sums, out):
    total = landed[0]
    for k in range(1, landed.shape[0]):
        total = total + landed[k]
    sums[...] = total
    wide = lax.dot_general(total, spread[...], NN, precision=highest, preferred_element_type=F32)
    lane = lax.broadcasted_iota(jnp.int32, (MODES, 8, 128), 2)
    first = lax.broadcasted_iota(jnp.int32, (MODES, 8, 128), 0)
    real = jnp.where((first == 0) & (lane % KX == 0), lifted[:, 1], 0.0)
    imag = jnp.zeros((MODES, 8, 128), F32)
    for f in range(FIELDS):
        one_re = wide[:MODES, f * 128 : (f + 1) * 128][:, None, :]
        one_im = wide[MODES:, f * 128 : (f + 1) * 128][:, None, :]
        weight_re = lifted[:, 2 * f]
        weight_im = lifted[:, 2 * f + 1]
        real = real + (one_re * weight_re - one_im * weight_im)
        imag = imag + (one_re * weight_im + one_im * weight_re)
    out[:, 0:8, :] = real
    out[:, 8:16, :] = imag


def by_kx(total, order):
    turned = total.T
    rows = jnp.zeros((KX, 2 * CHAN), F32)
    for f in range(4):
        rows = rows + lax.dot_general(
            turned[f * KX : (f + 1) * KX], order[f], NN, precision=highest, preferred_element_type=F32
        )
    return jnp.concatenate([rows[:MODES], rows[MODES:]], 1)


def owner_kernel(adjoint, scale, landed, weights, spread, order, sums, out):
    total = landed[0]
    for k in range(1, landed.shape[0]):
        total = total + landed[k]
    total = total * scale[0]
    wide = lax.dot_general(total, spread[...], NN, precision=highest, preferred_element_type=F32)
    real = jnp.zeros((8, 128), F32)
    imag = jnp.zeros((8, 128), F32)
    for i in range(CHAN):
        at, f = i // 4, i % 4
        one_re = wide[at : at + 1, f * 128 : (f + 1) * 128]
        one_im = wide[8 + at : 9 + at, f * 128 : (f + 1) * 128]
        weight_re = weights[i, 0]
        weight_im = weights[i, 1]
        if adjoint:
            real = real + (one_re * weight_re + one_im * weight_im)
            imag = imag + (one_im * weight_re - one_re * weight_im)
        else:
            real = real + (one_re * weight_re - one_im * weight_im)
            imag = imag + (one_re * weight_im + one_im * weight_re)
    for k in range(out.shape[0]):
        out[k, 0:8, :] = real
        out[k, 8:16, :] = imag
    sums[...] = by_kx(total, order)


def first_kernel(modes, fields, field_mix, field_shift, forward_y, inverse_y, blocks, slope, act, out, held, sums):
    step = pl.program_id(0)

    @pl.when(step == 0)
    def _():
        inverse_x(modes, doubled, blocks, held)

    pre = dot(held[step], inverse_y[...], TN).reshape(PER_GROUP, ROWS, NY)
    for c in range(PER_GROUP):
        value = pre[c] + field_shift[step * PER_GROUP + c]
        for f in range(FIELDS):
            value = value + field_mix[f, step * PER_GROUP + c] * fields[f]
        lifted, bent = gelu_terms(value)
        act[c] = lifted
        slope[c] = bent
    sums[step] = along_y(act[...].reshape(PER_GROUP * ROWS, NY), forward_y)

    @pl.when(step == GROUPS - 1)
    def _():
        write_modes(sums, blocks, out)


def second_kernel(modes, mixed, sensitivity, decoder, forward_y, inverse_y, blocks, grad, out, held, sums):
    step = pl.program_id(0)

    @pl.when(step == 0)
    def _():
        inverse_x(modes, doubled, blocks, held)

    pre = dot(held[step], inverse_y[...], TN).reshape(PER_GROUP, ROWS, NY)
    for c in range(PER_GROUP):
        _, bent = gelu_terms(pre[c] + mixed[c])
        grad[c] = bent * (decoder[step * PER_GROUP + c] * sensitivity[...])
    sums[step] = along_y(grad[...].reshape(PER_GROUP * ROWS, NY), forward_y)

    @pl.when(step == GROUPS - 1)
    def _():
        write_modes(sums, blocks, out)


def back_kernel(modes, mixed, slope, fields, pairs, forward_y, inverse_y, blocks, out, held, sums, cells, dots):
    step = pl.program_id(0)

    @pl.when(step == 0)
    def _():
        inverse_x(modes, lambda value: value * (1.0 / CELLS), blocks, held)
        dots[...] = jnp.zeros(dots.shape, F32)

    pre = dot(held[step], inverse_y[...], TN).reshape(PER_GROUP, ROWS, NY)
    lane = lax.broadcasted_iota(jnp.int32, (8, 128), 1)
    for c in range(PER_GROUP):
        value = (pre[c] + mixed[c]) * slope[c]
        cells[c] = value
        lines = []
        for f in range(FIELDS + 1):
            term = value if f == FIELDS else value * fields[f]
            term = (term[:, 0:128] + term[:, 128:256]) + (term[:, 256:384] + term[:, 384:512])
            term = (term[0:8] + term[8:16]) + (term[16:24] + term[24:32])
            lines.append(jnp.sum(term, axis=0, keepdims=True))
        lines.append(jnp.zeros((7 - FIELDS, 128), F32))
        total = jnp.sum(jnp.concatenate(lines, 0), axis=1, keepdims=True)
        dots[...] += jnp.where(lane == step * PER_GROUP + c, total, 0.0)
    sums[step] = along_y(cells[...].reshape(PER_GROUP * ROWS, NY), forward_y)

    @pl.when(step == GROUPS - 1)
    def _():
        write_modes(sums, blocks, out)
        for k in range(out.shape[0]):
            out[k, 16:24, :] = pairs[...]
            out[k, 24:32, :] = dots[...]


def picker():
    row = lax.broadcasted_iota(jnp.int32, (CHAN * 8, CHAN), 0)
    column = lax.broadcasted_iota(jnp.int32, (CHAN * 8, CHAN), 1)
    return jnp.where(row // 8 == column, 1.0, 0.0).astype(F32)


def same_row(value):
    row = lax.broadcasted_iota(jnp.int32, value.shape, 0)
    column = lax.broadcasted_iota(jnp.int32, value.shape, 1)
    return jnp.where(row % 8 == column % 8, value, 0.0)


def exact(left, right, dims):
    return lax.dot_general(left, right, dims, precision=highest, preferred_element_type=F32)


def mix_rows(cells, high_m, low_m, part):
    cells = cells[:, part * 8 : part * 8 + 8, :].reshape(CHAN * 8, NY)
    high, low = halves(cells)
    return high, low, dot(high_m, high, NN) + (dot(low_m, high, NN) + dot(high_m, low, NN))


def mix_kernel(act, matrix, shift, out):
    pick = picker()
    high_m, low_m = halves(same_row(exact(exact(pick, matrix[...], NT), pick, NT)))
    for part in range(ROWS // 8):
        _, _, mixed = mix_rows(act, high_m, low_m, part)
        mixed = mixed.reshape(CHAN, 8, NY)
        for c in range(CHAN):
            out[c, part * 8 : part * 8 + 8, :] = mixed[c] + shift[c]


def mix_back_kernel(grad, act, matrix, out, pairs):
    pick = picker()
    high_m, low_m = halves(same_row(exact(exact(pick, matrix[...], NN), pick, NT)))
    total = jnp.zeros((CHAN * 8, CHAN * 8), F32)
    for part in range(ROWS // 8):
        grad_high, grad_low, mixed = mix_rows(grad, high_m, low_m, part)
        out[:, part * 8 : part * 8 + 8, :] = mixed.reshape(CHAN, 8, NY)
        act_high, act_low = halves(act[:, part * 8 : part * 8 + 8, :].reshape(CHAN * 8, NY))
        total = total + (
            dot(act_high, grad_high, NT) + (dot(act_low, grad_high, NT) + dot(act_high, grad_low, NT))
        )
    total = exact(exact(pick, same_row(total), TN), pick, NN)
    pairs[...] = jnp.concatenate([total[8 * k : 8 * k + 8] for k in range(4)], 1)


def message_kernel(scale, landed, known, order, out):
    total = landed[0]
    for k in range(1, landed.shape[0]):
        total = total + landed[k]
    out[0:48, :] = known[...]
    out[48:64, :] = by_kx(total[0:16] * scale[0], order)
    out[64:80, :] = total[16:32]


def gradient_kernel(place, held, other, lift, spec, mix, planes):
    near = held.shape[0]
    for k in range(near):
        planes[k ^ place[0]] = held[k]
        planes[(k + near) ^ place[0]] = other[k]
    for layer, (at_in, at_out) in enumerate(((0, 48), (16, 32))):
        left = jnp.transpose(planes[:, at_in : at_in + MODES, :], (1, 0, 2))
        right = jnp.transpose(planes[:, at_out : at_out + MODES, :], (1, 0, 2))
        for k in range(MODES):
            high, low = halves(left[k])
            high_r, low_r = halves(right[k])
            both = dot(
                jnp.concatenate([high, low, high], 0), jnp.concatenate([high_r, high_r, low_r], 0), TN
            )
            for half in range(2):
                lane = half * 2 * CHAN
                block = both[lane : lane + 2 * CHAN, lane : lane + 2 * CHAN]
                kx = half * MODES + k
                spec[layer, 0, kx, 0] = block[:CHAN, :CHAN] + block[CHAN:, CHAN:]
                spec[layer, 0, kx, 1] = block[:CHAN, CHAN:] - block[CHAN:, :CHAN]
    total = planes[0, 64:80, :]
    for k in range(1, 2 * near):
        total = total + planes[k, 64:80, :]
    scale = 1.0 / math.sqrt(CELLS)
    mix[0] = exact(lift[...], total[8:16, :CHAN], TN) * scale
    for k in range(4):
        mix[1, 8 * k : 8 * k + 8, :] = total[0:8, CHAN * k : CHAN * (k + 1)] * scale


def whole(shape):
    return pl.BlockSpec(shape, lambda g: (0,) * len(shape))


def stepped(shape, at):
    return pl.BlockSpec(shape, lambda g: tuple(g if k == at else 0 for k in range(len(shape))))


SCALARS = pl.BlockSpec(memory_space=pltpu.SMEM)
MODE_SPEC = pl.BlockSpec((MODES, 16, 128), lambda g: (0, 0, 0))
CELL_SPEC = stepped((PER_GROUP, ROWS, NY), 0)
MODE_SHAPE = jax.ShapeDtypeStruct((MODES, 16, 128), F32)
LAYER_SCRATCH = (
    pltpu.VMEM((GROUPS, 6 * MODES, PER_GROUP * ROWS), BF16),
    pltpu.VMEM((GROUPS, 2 * MODES, PER_GROUP * ROWS), F32),
)
CELL_SHAPE = jax.ShapeDtypeStruct((CHAN, ROWS, NY), F32)


def layer_call(kernel, name, in_specs, out_specs, out_shape, scratch=()):
    return pl.pallas_call(
        kernel,
        name=name,
        grid=(GROUPS,),
        in_specs=in_specs,
        out_specs=out_specs,
        out_shape=out_shape,
        scratch_shapes=scratch,
        compiler_params=pltpu.CompilerParams(vmem_limit_bytes=VMEM_LIMIT),
        cost_estimate=pl.CostEstimate(flops=2 * 10**9, bytes_accessed=6 * 2**20, transcendentals=2**19),
    )


def plain_call(kernel, name, out_shape, scalar_args=(), count=0, flops=10**6, scratch=()):
    specs = [
        SCALARS if k in scalar_args else pl.BlockSpec(memory_space=pltpu.VMEM) for k in range(count)
    ]
    return pl.pallas_call(
        kernel,
        name=name,
        in_specs=specs,
        out_shape=out_shape,
        scratch_shapes=scratch,
        compiler_params=pltpu.CompilerParams(vmem_limit_bytes=VMEM_LIMIT),
        cost_estimate=pl.CostEstimate(flops=flops, bytes_accessed=4 * 2**20, transcendentals=0),
    )


def sum_blocks(rows, axis):
    return lax.all_to_all(rows, axis, split_axis=0, concat_axis=0, tiled=True)


def all_copies(block, count):
    return jnp.broadcast_to(block[None], (count,) + block.shape)


def gather_planes(block):
    held = block[None]
    for axis, bit in (("gy", 4), ("gy", 2), ("gy", 1)):
        count = lax.axis_size(axis)
        other = lax.ppermute(held, axis, [(i, i ^ bit) for i in range(count)])
        held = jnp.concatenate([held, other], 0)
    return held, lax.ppermute(held, "grp", [(0, 1), (1, 0)])


def shards(
    present_displacement,
    prior_displacement,
    fracture_state,
    grid_material_region,
    region_young_stiffness,
    borehole_grid_position,
    detonation_order,
    explosive_mass,
    output_loss_sensitivity,
    encoder_matrix,
    encoder_offset,
    fourier_mode_kernel,
    local_mixing_matrix,
    local_mixing_offset,
    decoder_matrix,
):
    depth, local_x, _ = present_displacement.shape
    at_x, at_z = lax.axis_index("gx"), lax.axis_index("grp")
    place = jnp.stack([at_z, lax.axis_index(("gx", "gy"))]).astype(jnp.int32)
    edge = jnp.where(at_z == 0, present_displacement[depth - 1 :], present_displacement[:1])
    over = lax.ppermute(edge, "grp", [(0, 1), (1, 0)])
    along = ("gx", "gy")
    ends = lax.axis_size(along) - 1
    above = lax.ppermute(present_displacement[:, local_x - 1 :], along, [(i, i + 1) for i in range(ends)])
    below = lax.ppermute(present_displacement[:, :1], along, [(i + 1, i) for i in range(ends)])
    charge = explosive_mass * jnp.power(borehole_attenuation, detonation_order.astype(F32))
    block_shape = jax.ShapeDtypeStruct(present_displacement.shape, F32)
    base, stiffness = plain_call(
        before_kernel, "before", (block_shape, block_shape), scalar_args=(0, 1, 2, 3), count=8
    )(
        place,
        region_young_stiffness,
        borehole_grid_position,
        charge,
        present_displacement,
        prior_displacement,
        fracture_state,
        grid_material_region,
    )
    advanced_displacement, advanced_fracture_state, message = plain_call(
        solver_kernel,
        "solver",
        (block_shape, block_shape, jax.ShapeDtypeStruct((depth, FIELDS, local_x, NY), F32)),
        scalar_args=(0,),
        count=8,
        scratch=(pltpu.VMEM((depth, 8, NY), F32),),
    )(place, present_displacement, over, above, below, base, stiffness, fracture_state)
    weights_0 = fourier_mode_kernel[0, 0]
    at_mean = (jnp.arange(KX) == 0) & (at_x == 0)
    matrix = jnp.concatenate([encoder_matrix, encoder_offset[None]], 0)
    lifted = jnp.einsum("fi,krio->frok", matrix, weights_0, precision=highest)
    slots = jnp.where(at_mean, lifted[FIELDS, 0], lifted[0, 1])
    lifted = lifted[:FIELDS].at[0, 1].set(slots).reshape(2 * FIELDS, 8, 128)
    lifted = sum_blocks(all_copies(lifted, MODES), "gx")
    message, lifted = lax.optimization_barrier((message, lifted))
    landed = lax.all_to_all(message, "gy", split_axis=0, concat_axis=0, tiled=True)

    table_fy, table_iy, table_x = wave_tables()
    forward_y = jnp.asarray(table_fy)
    inverse_y = jnp.asarray(table_iy)
    blocks = block_tables(jnp.asarray(table_x))
    spread = np.zeros((128, FIELDS, 4, KX), np.float32)
    for f in range(4):
        for k in range(KX):
            spread[f * KX + k, f, :, k] = 1.0
    spread = jnp.asarray(spread.reshape(128, 512))
    order = np.zeros((4, 2, 8, 2, 8, 4), np.float32)
    for f in range(4):
        for k in range(8):
            for part in range(2):
                order[f, part, k, part, k, f] = 1.0
    order = jnp.asarray(order.reshape(4, 16, 64))
    weights_1 = fourier_mode_kernel[1, 0]
    by_input = jnp.transpose(weights_1, (2, 1, 3, 0)).reshape(CHAN, 2, 8, 128)
    by_output = jnp.transpose(weights_1, (3, 1, 2, 0)).reshape(CHAN, 2, 8, 128)
    mix_0, mix_1 = local_mixing_matrix[0], local_mixing_matrix[1]
    field_mix = jnp.dot(encoder_matrix, mix_0, precision=highest)
    field_shift = jnp.dot(encoder_offset, mix_0, precision=highest) + local_mixing_offset[0]

    fields, field_modes = plain_call(
        field_kernel,
        "fields",
        (
            jax.ShapeDtypeStruct((FIELDS, ROWS, NY), F32),
            jax.ShapeDtypeStruct((MODES, 2 * MODES, 128), F32),
        ),
        count=3,
    )(landed, forward_y, blocks)
    landed = sum_blocks(field_modes, "gx")
    field_sums, modes = plain_call(
        lift_kernel, "lift", (jax.ShapeDtypeStruct((2 * MODES, 128), F32), MODE_SHAPE), count=3
    )(landed, lifted, spread)
    slope_0, act_1, partial = layer_call(
        first_kernel,
        "first",
        [
            MODE_SPEC,
            whole((FIELDS, ROWS, NY)),
            SCALARS,
            SCALARS,
            whole(forward_y.shape),
            whole(inverse_y.shape),
            whole(blocks.shape),
        ],
        [CELL_SPEC, CELL_SPEC, MODE_SPEC],
        [CELL_SHAPE, CELL_SHAPE, MODE_SHAPE],
        LAYER_SCRATCH,
    )(modes, fields, field_mix, field_shift, forward_y, inverse_y, blocks)

    owner_shapes = (jax.ShapeDtypeStruct((16, 128), F32), MODE_SHAPE)
    m_ky = jnp.where(at_x == 0, 1.0, 2.0).astype(F32)[None]

    def owner(adjoint, landed, weights):
        def kernel(*refs):
            owner_kernel(adjoint, *refs)

        name = "owner_back" if adjoint else "owner"
        scale = m_ky if adjoint else jnp.full((1,), 1.0 / CELLS, F32)
        sums, out = plain_call(kernel, name, owner_shapes, scalar_args=(0,), count=5)(
            scale, landed, weights, spread, order
        )
        return sums, sum_blocks(out, "gx")

    landed = sum_blocks(partial, "gx")
    mixed = plain_call(mix_kernel, "mix", CELL_SHAPE, scalar_args=(2,), count=3, flops=10**9)(
        act_1, mix_1, local_mixing_offset[1]
    )
    modes_1, modes = owner(False, landed, by_input)
    grad_1, partial = layer_call(
        second_kernel,
        "second",
        [
            MODE_SPEC,
            CELL_SPEC,
            whole((ROWS, NY)),
            SCALARS,
            whole(forward_y.shape),
            whole(inverse_y.shape),
            whole(blocks.shape),
        ],
        [CELL_SPEC, MODE_SPEC],
        [CELL_SHAPE, MODE_SHAPE],
        LAYER_SCRATCH,
    )(modes, mixed, output_loss_sensitivity[0], decoder_matrix, forward_y, inverse_y, blocks)

    landed = sum_blocks(partial, "gx")
    mixed, pairs_1 = plain_call(
        mix_back_kernel,
        "mix_back",
        (CELL_SHAPE, jax.ShapeDtypeStruct((8, 128), F32)),
        count=3,
        flops=2 * 10**9,
    )(grad_1, act_1, mix_1)
    back_1, modes = owner(True, landed, by_output)
    partial = layer_call(
        back_kernel,
        "back",
        [
            MODE_SPEC,
            CELL_SPEC,
            CELL_SPEC,
            whole((FIELDS, ROWS, NY)),
            whole((8, 128)),
            whole(forward_y.shape),
            whole(inverse_y.shape),
            whole(blocks.shape),
        ],
        whole((MODES, 32, 128)),
        jax.ShapeDtypeStruct((MODES, 32, 128), F32),
        LAYER_SCRATCH + (pltpu.VMEM((PER_GROUP, ROWS, NY), F32), pltpu.VMEM((8, 128), F32)),
    )(modes, mixed, slope_0, fields, pairs_1, forward_y, inverse_y, blocks)

    landed = sum_blocks(partial, "gx")
    own_fields = lax.dynamic_slice_in_dim(field_sums.reshape(2, MODES, FIELDS, KX), at_x, 1, 1)[:, 0]
    modes_0 = jnp.einsum("rfk,fi->kri", own_fields, encoder_matrix, precision=highest)
    modes_0 = modes_0.at[:, 0].add(jnp.where(at_mean, 1.0, 0.0)[:, None] * encoder_offset[None, :])
    modes_0 = modes_0.reshape(2, MODES, 2 * CHAN)
    modes_0 = jnp.concatenate([modes_0[0], modes_0[1]], 1)
    known = jnp.concatenate([modes_0, modes_1, back_1], 0)
    message = plain_call(
        message_kernel, "message", jax.ShapeDtypeStruct((80, 128), F32), scalar_args=(0,), count=4
    )(m_ky, landed, known, order)
    held, other = gather_planes(message)
    at_y = lax.axis_index("gy")
    slot = at_y // 4 + 2 * (at_y // 2 % 2) + 4 * (at_y % 2) + 8 * at_z
    lift = jnp.concatenate([encoder_matrix, encoder_offset[None], jnp.zeros((3, CHAN), F32)], 0)
    spec_grad, mix_grad = plain_call(
        gradient_kernel,
        "gradients",
        (
            jax.ShapeDtypeStruct((LAYERS, 1, KX, 2, CHAN, CHAN), F32),
            jax.ShapeDtypeStruct((LAYERS, CHAN, CHAN), F32),
        ),
        scalar_args=(0,),
        count=4,
        scratch=(pltpu.VMEM((16, 80, 128), F32),),
    )(slot.astype(jnp.int32)[None], held, other, lift)
    return advanced_displacement, advanced_fracture_state, spec_grad, mix_grad


def solution(mesh):
    return jax.shard_map(
        shards,
        mesh=mesh,
        in_specs=(
            P("grp", ("gx", "gy"), None),
            P("grp", ("gx", "gy"), None),
            P("grp", ("gx", "gy"), None),
            P("grp", ("gx", "gy"), None),
            P(),
            P(),
            P(),
            P(),
            P(("grp", "gy"), "gx", None),
            P(),
            P(),
            P(None, "gx", None, None, None, None),
            P(),
            P(),
            P(),
        ),
        out_specs=(
            P("grp", ("gx", "gy"), None),
            P("grp", ("gx", "gy"), None),
            P(None, "gx", None, None, None, None),
            P(),
        ),
        check_vma=False,
    )
```

```python
import math

import jax
import jax.numpy as jnp
import ml_dtypes
import numpy as np
from jax import lax
from jax.experimental import pallas as pl
from jax.experimental.pallas import tpu as pltpu
from jax.sharding import PartitionSpec as P

NX = 512
NY = 512
MODES = 16
CHAN = 32
FIELDS = 4
LAYERS = 2
GROUPS = 4
PER_GROUP = CHAN // GROUPS
ROWS = 32
KX = 2 * MODES
CELLS = NX * NY

highest = lax.Precision.HIGHEST
split = lax.Precision.HIGH
courant = 0.08
damage_rate = 0.5
strain_limit = 1.0
borehole_attenuation = 0.95
F32 = jnp.float32
BF16 = jnp.bfloat16
NN = (((1,), (0,)), ((), ()))
NT = (((1,), (1,)), ((), ()))
TN = (((0,), (0,)), ((), ()))
GELU_A = math.sqrt(2.0 / math.pi)
GELU_B = 0.044715
SMALL_LIMIT = 24 * 1024 * 1024
LARGE_LIMIT = 62 * 1024 * 1024


def parts_of(table, count):
    parts = []
    for _ in range(count):
        part = table.astype(ml_dtypes.bfloat16)
        parts.append(part)
        table = table - part.astype(np.float64)
    return parts


def wave_tables():
    ky = np.arange(MODES)
    angle_y = 2.0 * np.pi / NY * (ky[:, None] * np.arange(NY)[None, :] % NY)
    along_y = np.concatenate([np.cos(angle_y), -np.sin(angle_y)], 0)
    kx = np.concatenate([np.arange(MODES), NX - MODES + np.arange(MODES)])
    angle_x = 2.0 * np.pi / NX * (np.arange(NX)[:, None] * kx[None, :] % NX)
    y1, y2, y3 = parts_of(along_y, 3)
    forward_y = np.concatenate([y1, y2, y3], 0)
    inverse_y = np.concatenate([y1, y1, y2], 0)
    c1, c2 = parts_of(np.cos(angle_x), 2)
    s1, s2 = parts_of(np.sin(angle_x), 2)
    return forward_y, inverse_y, np.stack([c1, s1, c2, s2], 0)


def block_tables(along_x):
    local = lax.dynamic_slice_in_dim(along_x, lax.axis_index("gx") * ROWS, ROWS, 1)
    eye = jnp.eye(PER_GROUP, dtype=BF16)
    wide = eye[:, None, None, :, None] * jnp.transpose(local, (1, 0, 2))[None, :, :, None, :]
    return wide.reshape(PER_GROUP * ROWS, 4 * PER_GROUP * KX)


def halves(value):
    high = value.astype(BF16)
    return high, (value - high.astype(F32)).astype(BF16)


def dot(left, right, dims):
    return lax.dot_general(left, right, dims, preferred_element_type=F32)


def along_y(cells, forward_y):
    high, low = halves(cells)
    first = dot(forward_y[...], high, NT)
    second = dot(forward_y[: 4 * MODES, :], low, NT)
    return first[: 2 * MODES] + (
        first[2 * MODES : 4 * MODES]
        + first[4 * MODES :]
        + second[: 2 * MODES]
        + second[2 * MODES :]
    )


def along_x(pieces, blocks, dims, width):
    count = len(pieces)
    rows = 2 * MODES * count
    stacked = jnp.concatenate(halves(jnp.concatenate(pieces, 0)), 0)
    span = PER_GROUP * KX
    table = [blocks[:width, k * span : k * span + width] for k in range(4)]
    cos_1, sin_1 = [dot(stacked, part, dims) for part in table[:2]]
    cos_2, sin_2 = [dot(stacked[:rows], part, dims) for part in table[2:]]
    cos = cos_1[:rows] + (cos_1[rows:] + cos_2)
    sin = sin_1[:rows] + (sin_1[rows:] + sin_2)
    cut = [slice(2 * MODES * k, 2 * MODES * (k + 1)) for k in range(count)]
    return [(cos[at], sin[at]) for at in cut]


def forward_x(pieces, blocks, width):
    return [
        (cos[:MODES] + sin[MODES:], cos[MODES:] - sin[:MODES])
        for cos, sin in along_x(pieces, blocks, NN, width)
    ]


def inverse_x(modes, scaled, blocks, held):
    pieces = []
    for g in range(GROUPS):
        real = jnp.concatenate([modes[:, 2 * g, :], modes[:, 2 * g + 1, :]], 1)
        imag = jnp.concatenate([modes[:, 8 + 2 * g, :], modes[:, 9 + 2 * g, :]], 1)
        pieces.append(jnp.concatenate([scaled(real), scaled(imag)], 0))
    for g, (cos, sin) in enumerate(along_x(pieces, blocks, NT, PER_GROUP * ROWS)):
        rows = jnp.concatenate([cos[:MODES] - sin[MODES:], cos[MODES:] + sin[:MODES]], 0)
        high, low = halves(rows)
        held[g] = jnp.concatenate([high, low, high], 0)


def write_modes(sums, blocks, out):
    pieces = [sums[g] for g in range(GROUPS)]
    for g, (real, imag) in enumerate(forward_x(pieces, blocks, PER_GROUP * ROWS)):
        out[:, 2 * g, :] = real[:, :128]
        out[:, 2 * g + 1, :] = real[:, 128:]
        out[:, 8 + 2 * g, :] = imag[:, :128]
        out[:, 9 + 2 * g, :] = imag[:, 128:]


def doubled(value):
    row = lax.broadcasted_iota(jnp.int32, value.shape, 0)
    return jnp.where(row == 0, value, 2.0 * value)


def gelu_terms(value):
    square = value * value
    bend = jnp.tanh(value * (GELU_A + (GELU_A * GELU_B) * square))
    half = 0.5 + 0.5 * bend
    slope = half + (value * (1.0 - bend * bend)) * (0.5 * GELU_A + (1.5 * GELU_A * GELU_B) * square)
    return value * half, slope


def before_kernel(place, stiff, position, charge, now, prior, fracture, region, base, stiffness):
    zones = region[...]
    modulus = jnp.zeros(zones.shape, F32)
    for k in range(stiff.shape[0]):
        modulus = jnp.where(zones == k, stiff[k], modulus)
    stiffness[...] = modulus * (1.0 - fracture[...])
    depth, rows, _ = now.shape
    cell = (
        (place[0] * depth + lax.broadcasted_iota(jnp.int32, now.shape, 0)) * CELLS
        + (place[1] * rows + lax.broadcasted_iota(jnp.int32, now.shape, 1)) * NY
        + lax.broadcasted_iota(jnp.int32, now.shape, 2)
    )
    source = jnp.zeros(now.shape, F32)
    for h in range(position.shape[0]):
        source = source + jnp.where(cell == position[h], charge[h], 0.0)
    base[...] = 2.0 * now[...] - prior[...] + source


def solver_kernel(place, now, over, above, below, base, stiffness, fracture, ahead, damage, fields, wide):
    depth, rows, _ = now.shape
    wide[...] = jnp.zeros(wide.shape, F32)
    wide[:, 1:2, :] = above[...]
    wide[:, 2 : 2 + rows, :] = now[...]
    wide[:, 2 + rows : 3 + rows, :] = below[...]
    upper = place[0] == 1
    lane = lax.broadcasted_iota(jnp.int32, (rows, NY), 1)
    for z in range(depth):
        here = now[z]
        other = over[0]
        before_z = now[z - 1] if z > 0 else jnp.where(upper, other, 0.0)
        after_z = now[z + 1] if z < depth - 1 else jnp.where(upper, 0.0, other)
        before_x = wide[z, 1 : 1 + rows, :]
        after_x = wide[z, 3 : 3 + rows, :]
        before_y = jnp.where(lane == 0, 0.0, pltpu.roll(here, 1, 1))
        after_y = jnp.where(lane == NY - 1, 0.0, pltpu.roll(here, NY - 1, 1))
        laplace = after_z + before_z + after_x + before_x + after_y + before_y - 6.0 * here
        strain_z = 0.5 * (after_z - before_z)
        strain_x = 0.5 * (after_x - before_x)
        strain_y = 0.5 * (after_y - before_y)
        stiff = stiffness[z]
        moved = base[z] + courant * stiff * laplace
        square = strain_x * strain_x + strain_y * strain_y + strain_z * strain_z
        broken = fracture[z]
        grown = broken + (1.0 - broken) * jnp.tanh(
            damage_rate * jnp.maximum(square - strain_limit, 0.0)
        )
        ahead[z] = moved
        damage[z] = grown
        fields[z, 0] = moved
        fields[z, 1] = grown
        fields[z, 2] = stiff * strain_x
        fields[z, 3] = stiff * strain_y


def field_kernel(landed, forward_y, blocks, fields, out):
    blocks_in, _, rows, _ = landed.shape
    for k in range(blocks_in):
        for f in range(FIELDS):
            fields[f, k * rows : (k + 1) * rows, :] = landed[k, f]
    sums = along_y(fields[...].reshape(FIELDS * ROWS, NY), forward_y)
    ((real, imag),) = forward_x([sums], blocks, FIELDS * ROWS)
    for k in range(out.shape[0]):
        out[k, :MODES, :] = real * (1.0 / CELLS)
        out[k, MODES:, :] = imag * (1.0 / CELLS)


def sum_of(landed):
    parts = [landed[k] for k in range(landed.shape[0])]
    while len(parts) > 1:
        parts = [left + right for left, right in zip(parts[::2], parts[1::2])]
    return parts[0]


def lift_kernel(place, landed, own, other, spread, sums, out):
    total = sum_of(landed)
    sums[...] = total
    wide = exact(total, spread[...], NN)
    upper = place[0] == 1
    lane = lax.broadcasted_iota(jnp.int32, (MODES, 8, 128), 2)
    first = lax.broadcasted_iota(jnp.int32, (MODES, 8, 128), 0)
    shift = jnp.where(upper, other[:, 1], own[:, 1])
    real = jnp.where((first == 0) & (lane % KX == 0), shift, 0.0)
    imag = jnp.zeros((MODES, 8, 128), F32)
    for f in range(FIELDS):
        k = 2 * (f % 2)
        near = upper if f >= 2 else jnp.logical_not(upper)
        weight_re = jnp.where(near, own[:, k], other[:, k])
        weight_im = jnp.where(near, own[:, k + 1], other[:, k + 1])
        one_re = wide[:MODES, f * 128 : (f + 1) * 128][:, None, :]
        one_im = wide[MODES:, f * 128 : (f + 1) * 128][:, None, :]
        real = real + (one_re * weight_re - one_im * weight_im)
        imag = imag + (one_re * weight_im + one_im * weight_re)
    out[:, 0:8, :] = real
    out[:, 8:16, :] = imag


def by_kx(total, order):
    turned = total.T
    rows = jnp.zeros((KX, 2 * CHAN), F32)
    for f in range(4):
        rows = rows + lax.dot_general(
            turned[f * KX : (f + 1) * KX], order[f], NN, precision=highest, preferred_element_type=F32
        )
    return jnp.concatenate([rows[:MODES], rows[MODES:]], 1)


def apply_weights(adjoint, total, weights, spread, order, sums, out):
    wide = exact(total, spread[...], NN)
    real = jnp.zeros((8, 128), F32)
    imag = jnp.zeros((8, 128), F32)
    for i in range(CHAN):
        at, f = i // 4, i % 4
        one_re = wide[at : at + 1, f * 128 : (f + 1) * 128]
        one_im = wide[8 + at : 9 + at, f * 128 : (f + 1) * 128]
        weight_re = weights[i, 0]
        weight_im = weights[i, 1]
        if adjoint:
            real = real + (one_re * weight_re + one_im * weight_im)
            imag = imag + (one_im * weight_re - one_re * weight_im)
        else:
            real = real + (one_re * weight_re - one_im * weight_im)
            imag = imag + (one_re * weight_im + one_im * weight_re)
    for k in range(out.shape[0]):
        out[k, 0:8, :] = real
        out[k, 8:16, :] = imag
    sums[...] = by_kx(total, order)


def owner_kernel(adjoint, scale, landed, weights, spread, order, sums, out):
    total = sum_of(landed) * scale[0]
    apply_weights(adjoint, total, weights, spread, order, sums, out)


def group_of(ref, g):
    return ref.at[g * PER_GROUP : (g + 1) * PER_GROUP]


def part_of(ref, part):
    return ref.at[:, part * 8 : part * 8 + 8, :]


def copies(source, target, sems, cut):
    return [pltpu.make_async_copy(cut(source, k), cut(target, k), sems.at[k]) for k in range(GROUPS)]


def first_kernel(
    modes, fields, field_mix, field_shift, forward_y, inverse_y, blocks, slope_out, act_out, out, held, sums, slope, act, sems
):
    leaving = copies(slope, slope_out, sems.at[0], group_of)
    beside = copies(act, act_out, sems.at[1], group_of)
    inverse_x(modes, doubled, blocks, held)
    for g in range(GROUPS):
        pre = dot(held[g], inverse_y[...], TN).reshape(PER_GROUP, ROWS, NY)
        for k in range(PER_GROUP):
            c = g * PER_GROUP + k
            value = pre[k] + field_shift[c]
            for f in range(FIELDS):
                value = value + field_mix[f, c] * fields[f]
            act[c], slope[c] = gelu_terms(value)
        leaving[g].start()
        beside[g].start()
        cells = act[g * PER_GROUP : (g + 1) * PER_GROUP].reshape(PER_GROUP * ROWS, NY)
        sums[g] = along_y(cells, forward_y)
    write_modes(sums, blocks, out)
    for copy in leaving + beside:
        copy.wait()


def second_kernel(
    modes, mixed_in, sensitivity, decoder, forward_y, inverse_y, blocks, grad_out, out, held, sums, mixed, grad, sems
):
    coming = copies(mixed_in, mixed, sems.at[0], group_of)
    leaving = copies(grad, grad_out, sems.at[1], group_of)
    for copy in coming:
        copy.start()
    inverse_x(modes, doubled, blocks, held)
    for g in range(GROUPS):
        pre = dot(held[g], inverse_y[...], TN).reshape(PER_GROUP, ROWS, NY)
        coming[g].wait()
        for k in range(PER_GROUP):
            c = g * PER_GROUP + k
            _, slope = gelu_terms(pre[k] + mixed[c])
            grad[c] = slope * (decoder[c] * sensitivity[...])
        leaving[g].start()
        cells = grad[g * PER_GROUP : (g + 1) * PER_GROUP].reshape(PER_GROUP * ROWS, NY)
        sums[g] = along_y(cells, forward_y)
    write_modes(sums, blocks, out)
    for copy in leaving:
        copy.wait()


def back_kernel(
    modes, mixed_in, slope_in, fields, pairs, forward_y, inverse_y, blocks, out, held, sums, mixed, slope, cells, sems
):
    coming = copies(mixed_in, mixed, sems.at[0], group_of)
    beside = copies(slope_in, slope, sems.at[1], group_of)
    for g in range(GROUPS):
        coming[g].start()
        beside[g].start()
    inverse_x(modes, lambda value: value * (1.0 / CELLS), blocks, held)
    lane = lax.broadcasted_iota(jnp.int32, (8, 128), 1)
    dots = jnp.zeros((8, 128), F32)
    for g in range(GROUPS):
        pre = dot(held[g], inverse_y[...], TN).reshape(PER_GROUP, ROWS, NY)
        coming[g].wait()
        beside[g].wait()
        for k in range(PER_GROUP):
            c = g * PER_GROUP + k
            value = (pre[k] + mixed[c]) * slope[c]
            cells[g % 2, k] = value
            lines = []
            for f in range(FIELDS + 1):
                term = value if f == FIELDS else value * fields[f]
                term = (term[:, 0:128] + term[:, 128:256]) + (term[:, 256:384] + term[:, 384:512])
                term = (term[0:8] + term[8:16]) + (term[16:24] + term[24:32])
                lines.append(jnp.sum(term, axis=0, keepdims=True))
            lines.append(jnp.zeros((7 - FIELDS, 128), F32))
            total = jnp.sum(jnp.concatenate(lines, 0), axis=1, keepdims=True)
            dots = jnp.where(lane == c, total, dots)
        sums[g] = along_y(cells[g % 2].reshape(PER_GROUP * ROWS, NY), forward_y)
    write_modes(sums, blocks, out)
    for k in range(out.shape[0]):
        out[k, 16:24, :] = pairs[...]
        out[k, 24:32, :] = dots


def picker():
    row = lax.broadcasted_iota(jnp.int32, (CHAN * 8, CHAN), 0)
    column = lax.broadcasted_iota(jnp.int32, (CHAN * 8, CHAN), 1)
    return jnp.where(row // 8 == column, 1.0, 0.0).astype(F32)


def same_row(value):
    row = lax.broadcasted_iota(jnp.int32, value.shape, 0)
    column = lax.broadcasted_iota(jnp.int32, value.shape, 1)
    return jnp.where(row % 8 == column % 8, value, 0.0)


def exact(left, right, dims):
    return lax.dot_general(left, right, dims, precision=highest, preferred_element_type=F32)


def mix_rows(cells, high_m, low_m, part):
    cells = cells[:, part * 8 : part * 8 + 8, :].reshape(CHAN * 8, NY)
    high, low = halves(cells)
    return high, low, dot(high_m, high, NN) + (dot(low_m, high, NN) + dot(high_m, low, NN))


def mix_kernel(act_in, matrix, shift, out, act, mixed, sems):
    coming = copies(act_in, act, sems.at[0], part_of)
    leaving = copies(mixed, out, sems.at[1], part_of)
    for copy in coming:
        copy.start()
    pick = picker()
    high_m, low_m = halves(same_row(exact(exact(pick, matrix[...], NT), pick, NT)))
    for part in range(ROWS // 8):
        coming[part].wait()
        _, _, sums = mix_rows(act, high_m, low_m, part)
        sums = sums.reshape(CHAN, 8, NY)
        for c in range(CHAN):
            mixed[c, part * 8 : part * 8 + 8, :] = sums[c] + shift[c]
        leaving[part].start()
    for copy in leaving:
        copy.wait()


def mix_back_kernel(grad_in, act_in, matrix, out, pairs, grad, act, mixed, sems):
    coming = copies(grad_in, grad, sems.at[0], part_of)
    leaving = copies(mixed, out, sems.at[1], part_of)
    beside = copies(act_in, act, sems.at[2], part_of)
    for part in range(GROUPS):
        coming[part].start()
        beside[part].start()
    pick = picker()
    high_m, low_m = halves(same_row(exact(exact(pick, matrix[...], NN), pick, NT)))
    total = jnp.zeros((CHAN * 8, CHAN * 8), F32)
    for part in range(ROWS // 8):
        coming[part].wait()
        grad_high, grad_low, sums = mix_rows(grad, high_m, low_m, part)
        mixed[:, part * 8 : part * 8 + 8, :] = sums.reshape(CHAN, 8, NY)
        leaving[part].start()
        beside[part].wait()
        act_high, act_low = halves(act[:, part * 8 : part * 8 + 8, :].reshape(CHAN * 8, NY))
        total = total + (
            dot(act_high, grad_high, NT) + (dot(act_low, grad_high, NT) + dot(act_high, grad_low, NT))
        )
    total = exact(exact(pick, same_row(total), TN), pick, NN)
    pairs[...] = jnp.concatenate([total[8 * k : 8 * k + 8] for k in range(4)], 1)
    for copy in leaving:
        copy.wait()


def message_kernel(scale, landed, known, order, out):
    total = sum_of(landed)
    out[0:48, :] = known[...]
    out[48:64, :] = by_kx(total[0:16] * scale[0], order)
    out[64:80, :] = total[16:32]


def gradient_kernel(place, held, other, lift, spec, mix, planes):
    near = held.shape[0]
    for k in range(near):
        planes[k ^ place[0]] = held[k]
        planes[(k + near) ^ place[0]] = other[k]
    for layer, (at_in, at_out) in enumerate(((0, 48), (16, 32))):
        left = jnp.transpose(planes[:, at_in : at_in + MODES, :], (1, 0, 2)).reshape(16 * MODES, 128)
        right = jnp.transpose(planes[:, at_out : at_out + MODES, :], (1, 0, 2)).reshape(16 * MODES, 128)
        turned = [right] + [pltpu.roll(right, 128 - CHAN * j, 1) for j in (1, 2, 3)]
        turned = [halves(value) for value in turned]
        high_l, low_l = halves(left)
        for k in range(MODES):
            at = slice(16 * k, 16 * k + 16)
            stacked = jnp.concatenate([high_l[at], low_l[at], high_l[at]], 0)
            quarters = [
                dot(stacked, jnp.concatenate([high[at], high[at], low[at]], 0), TN)
                for high, low in turned
            ]
            for half in range(2):
                row = half * 2 * CHAN
                real, imag = quarters[2 * half], quarters[2 * half + 1]
                middle, end = row + CHAN, row + 2 * CHAN
                kx = half * MODES + k
                spec[layer, 0, kx, 0] = real[row:middle, :CHAN] + imag[middle:end, :CHAN]
                spec[layer, 0, kx, 1] = imag[row:middle, :CHAN] - real[middle:end, :CHAN]
    total = planes[0, 64:80, :]
    for k in range(1, 2 * near):
        total = total + planes[k, 64:80, :]
    scale = 1.0 / math.sqrt(CELLS)
    mix[0] = exact(lift[...], total[8:16, :CHAN], TN) * scale
    for k in range(4):
        mix[1, 8 * k : 8 * k + 8, :] = total[0:8, CHAN * k : CHAN * (k + 1)] * scale


SCALARS = pl.BlockSpec(memory_space=pltpu.SMEM)
MODE_SHAPE = jax.ShapeDtypeStruct((MODES, 16, 128), F32)
CELL_SHAPE = jax.ShapeDtypeStruct((CHAN, ROWS, NY), F32)
CELLS_VMEM = pltpu.VMEM((CHAN, ROWS, NY), F32)
LAYER_SCRATCH = (
    pltpu.VMEM((GROUPS, 6 * MODES, PER_GROUP * ROWS), BF16),
    pltpu.VMEM((GROUPS, 2 * MODES, PER_GROUP * ROWS), F32),
)


def local_call(kernel, name, out_shape, scalar_args=(), count=0, flops=10**6, scratch=(), far_args=(), far_outs=()):
    vmem = pl.BlockSpec(memory_space=pltpu.VMEM)
    far = pl.BlockSpec(memory_space=pltpu.HBM)
    single = not isinstance(out_shape, tuple)
    outs = [far if k in far_outs else vmem for k in range(1 if single else len(out_shape))]
    return pl.pallas_call(
        kernel,
        name=name,
        in_specs=[
            SCALARS if k in scalar_args else far if k in far_args else vmem for k in range(count)
        ],
        out_specs=outs[0] if single else outs,
        out_shape=out_shape,
        scratch_shapes=scratch,
        compiler_params=pltpu.CompilerParams(vmem_limit_bytes=LARGE_LIMIT if far_args or far_outs else SMALL_LIMIT),
        cost_estimate=pl.CostEstimate(flops=flops, bytes_accessed=4 * 2**20, transcendentals=0),
    )


def sum_blocks(rows, axis):
    return lax.all_to_all(rows, axis, split_axis=0, concat_axis=0, tiled=True)


def all_copies(block, count):
    return jnp.broadcast_to(block[None], (count,) + block.shape)


def gather_planes(block):
    held = block[None]
    for axis, bit in (("gy", 4), ("gy", 2), ("gy", 1)):
        count = lax.axis_size(axis)
        other = lax.ppermute(held, axis, [(i, i ^ bit) for i in range(count)])
        held = jnp.concatenate([held, other], 0)
    return held, lax.ppermute(held, "grp", [(0, 1), (1, 0)])


def shards(
    present_displacement,
    prior_displacement,
    fracture_state,
    grid_material_region,
    region_young_stiffness,
    borehole_grid_position,
    detonation_order,
    explosive_mass,
    output_loss_sensitivity,
    encoder_matrix,
    encoder_offset,
    fourier_mode_kernel,
    local_mixing_matrix,
    local_mixing_offset,
    decoder_matrix,
):
    depth, local_x, _ = present_displacement.shape
    at_x, at_z = lax.axis_index("gx"), lax.axis_index("grp")
    place = jnp.stack([at_z, lax.axis_index(("gx", "gy"))]).astype(jnp.int32)
    edge = jnp.where(at_z == 0, present_displacement[depth - 1 :], present_displacement[:1])
    over = lax.ppermute(edge, "grp", [(0, 1), (1, 0)])
    along = ("gx", "gy")
    ends = lax.axis_size(along) - 1
    above = lax.ppermute(present_displacement[:, local_x - 1 :], along, [(i, i + 1) for i in range(ends)])
    below = lax.ppermute(present_displacement[:, :1], along, [(i + 1, i) for i in range(ends)])
    charge = explosive_mass * jnp.power(borehole_attenuation, detonation_order.astype(F32))
    block_shape = jax.ShapeDtypeStruct(present_displacement.shape, F32)
    base, stiffness = local_call(
        before_kernel, "before", (block_shape, block_shape), scalar_args=(0, 1, 2, 3), count=8
    )(
        place,
        region_young_stiffness,
        borehole_grid_position,
        charge,
        present_displacement,
        prior_displacement,
        fracture_state,
        grid_material_region,
    )
    advanced_displacement, advanced_fracture_state, message = local_call(
        solver_kernel,
        "solver",
        (block_shape, block_shape, jax.ShapeDtypeStruct((depth, FIELDS, local_x, NY), F32)),
        scalar_args=(0,),
        count=8,
        scratch=(pltpu.VMEM((depth, 8, NY), F32),),
    )(place, present_displacement, over, above, below, base, stiffness, fracture_state)
    weights_0 = fourier_mode_kernel[0, 0]
    at_mean = (jnp.arange(KX) == 0) & (at_x == 0)
    matrix = jnp.concatenate([encoder_matrix, encoder_offset[None]], 0)
    lifted = jnp.einsum("fi,krio->frok", matrix, weights_0, precision=highest)
    slot = (jnp.arange(FIELDS * 2) == 1).reshape(FIELDS, 2, 1, 1) & at_mean
    lifted = jnp.where(slot, lifted[FIELDS, 0], lifted[:FIELDS])
    lifted = lifted.reshape(2, FIELDS, 8, 128)
    lifted = jnp.where(at_z == 0, lifted[0], lifted[1])
    lifted = sum_blocks(all_copies(lifted, MODES), "gx")
    message, lifted = lax.optimization_barrier((message, lifted))
    landed = lax.all_to_all(message, "gy", split_axis=0, concat_axis=0, tiled=True)
    lifted_other = lax.ppermute(lifted, "grp", [(0, 1), (1, 0)])

    table_fy, table_iy, table_x = wave_tables()
    forward_y = jnp.asarray(table_fy)
    inverse_y = jnp.asarray(table_iy)
    blocks = block_tables(jnp.asarray(table_x))
    spread = np.zeros((128, FIELDS, 4, KX), np.float32)
    for f in range(4):
        for k in range(KX):
            spread[f * KX + k, f, :, k] = 1.0
    spread = jnp.asarray(spread.reshape(128, 512))
    order = np.zeros((4, 2, 8, 2, 8, 4), np.float32)
    for f in range(4):
        for k in range(8):
            for part in range(2):
                order[f, part, k, part, k, f] = 1.0
    order = jnp.asarray(order.reshape(4, 16, 64))
    weights_1 = fourier_mode_kernel[1, 0]
    by_input = jnp.transpose(weights_1, (2, 1, 3, 0)).reshape(CHAN, 2, 8, 128)
    by_output = jnp.transpose(weights_1, (3, 1, 2, 0)).reshape(CHAN, 2, 8, 128)
    mix_0, mix_1 = local_mixing_matrix[0], local_mixing_matrix[1]
    field_mix = jnp.dot(encoder_matrix, mix_0, precision=highest)
    field_shift = jnp.dot(encoder_offset, mix_0, precision=highest) + local_mixing_offset[0]

    fields, field_modes = local_call(
        field_kernel,
        "fields",
        (
            jax.ShapeDtypeStruct((FIELDS, ROWS, NY), F32),
            jax.ShapeDtypeStruct((MODES, 2 * MODES, 128), F32),
        ),
        count=3,
    )(landed, forward_y, blocks)
    landed = sum_blocks(field_modes, "gx")
    field_sums, modes = local_call(
        lift_kernel,
        "lift",
        (jax.ShapeDtypeStruct((2 * MODES, 128), F32), MODE_SHAPE),
        scalar_args=(0,),
        count=5,
    )(place, landed, lifted, lifted_other, spread)
    slope_0, act_1, partial = local_call(
        first_kernel,
        "first",
        (CELL_SHAPE, CELL_SHAPE, MODE_SHAPE),
        scalar_args=(2, 3),
        count=7,
        flops=2 * 10**9,
        scratch=LAYER_SCRATCH + (CELLS_VMEM, CELLS_VMEM, pltpu.SemaphoreType.DMA((2, GROUPS))),
        far_outs=(0, 1),
    )(modes, fields, field_mix, field_shift, forward_y, inverse_y, blocks)

    owner_shapes = (jax.ShapeDtypeStruct((16, 128), F32), MODE_SHAPE)
    m_ky = jnp.where(at_x == 0, 1.0, 2.0).astype(F32)[None]

    def owner(adjoint, landed, weights):
        def kernel(*refs):
            owner_kernel(adjoint, *refs)

        name = "owner_back" if adjoint else "owner"
        scale = m_ky if adjoint else jnp.full((1,), 1.0 / CELLS, F32)
        sums, out = local_call(kernel, name, owner_shapes, scalar_args=(0,), count=5)(
            scale, landed, weights, spread, order
        )
        return sums, sum_blocks(out, "gx")

    landed = sum_blocks(partial, "gx")
    mixed = local_call(
        mix_kernel,
        "mix",
        CELL_SHAPE,
        scalar_args=(2,),
        count=3,
        flops=10**9,
        scratch=(CELLS_VMEM, CELLS_VMEM, pltpu.SemaphoreType.DMA((2, GROUPS))),
        far_args=(0,),
        far_outs=(0,),
    )(act_1, mix_1, local_mixing_offset[1])
    modes_1, modes = owner(False, landed, by_input)
    grad_1, partial = local_call(
        second_kernel,
        "second",
        (CELL_SHAPE, MODE_SHAPE),
        scalar_args=(3,),
        count=7,
        flops=2 * 10**9,
        scratch=LAYER_SCRATCH + (CELLS_VMEM, CELLS_VMEM, pltpu.SemaphoreType.DMA((2, GROUPS))),
        far_args=(1,),
        far_outs=(0,),
    )(modes, mixed, output_loss_sensitivity[0], decoder_matrix, forward_y, inverse_y, blocks)

    landed = sum_blocks(partial, "gx")
    mixed, pairs_1 = local_call(
        mix_back_kernel,
        "mix_back",
        (CELL_SHAPE, jax.ShapeDtypeStruct((8, 128), F32)),
        count=3,
        flops=2 * 10**9,
        scratch=(CELLS_VMEM, CELLS_VMEM, CELLS_VMEM, pltpu.SemaphoreType.DMA((3, GROUPS))),
        far_args=(0, 1),
        far_outs=(0,),
    )(grad_1, act_1, mix_1)
    back_1, modes = owner(True, landed, by_output)
    partial = local_call(
        back_kernel,
        "back",
        jax.ShapeDtypeStruct((MODES, 32, 128), F32),
        count=8,
        flops=2 * 10**9,
        scratch=LAYER_SCRATCH
        + (CELLS_VMEM, CELLS_VMEM, pltpu.VMEM((2, PER_GROUP, ROWS, NY), F32), pltpu.SemaphoreType.DMA((2, GROUPS))),
        far_args=(1, 2),
    )(modes, mixed, slope_0, fields, pairs_1, forward_y, inverse_y, blocks)

    landed = sum_blocks(partial, "gx")
    own_fields = lax.dynamic_slice_in_dim(field_sums.reshape(2, MODES, FIELDS, KX), at_x, 1, 1)[:, 0]
    modes_0 = jnp.einsum("rfk,fi->kri", own_fields, encoder_matrix, precision=highest)
    modes_0 = modes_0.at[:, 0].add(jnp.where(at_mean, 1.0, 0.0)[:, None] * encoder_offset[None, :])
    modes_0 = modes_0.reshape(2, MODES, 2 * CHAN)
    modes_0 = jnp.concatenate([modes_0[0], modes_0[1]], 1)
    known = jnp.concatenate([modes_0, modes_1, back_1], 0)
    message = local_call(
        message_kernel, "message", jax.ShapeDtypeStruct((80, 128), F32), scalar_args=(0,), count=4
    )(m_ky, landed, known, order)
    held, other = gather_planes(message)
    at_y = lax.axis_index("gy")
    slot = at_y // 4 + 2 * (at_y // 2 % 2) + 4 * (at_y % 2) + 8 * at_z
    lift = jnp.concatenate([encoder_matrix, encoder_offset[None], jnp.zeros((3, CHAN), F32)], 0)
    spec_grad, mix_grad = local_call(
        gradient_kernel,
        "gradients",
        (
            jax.ShapeDtypeStruct((LAYERS, 1, KX, 2, CHAN, CHAN), F32),
            jax.ShapeDtypeStruct((LAYERS, CHAN, CHAN), F32),
        ),
        scalar_args=(0,),
        count=4,
        scratch=(pltpu.VMEM((16, 80, 128), F32),),
    )(slot.astype(jnp.int32)[None], held, other, lift)
    return advanced_displacement, advanced_fracture_state, spec_grad, mix_grad


def solution(mesh):
    return jax.shard_map(
        shards,
        mesh=mesh,
        in_specs=(
            P("grp", ("gx", "gy"), None),
            P("grp", ("gx", "gy"), None),
            P("grp", ("gx", "gy"), None),
            P("grp", ("gx", "gy"), None),
            P(),
            P(),
            P(),
            P(),
            P(("grp", "gy"), "gx", None),
            P(),
            P(),
            P(None, "gx", None, None, None, None),
            P(),
            P(),
            P(),
        ),
        out_specs=(
            P("grp", ("gx", "gy"), None),
            P("grp", ("gx", "gy"), None),
            P(None, "gx", None, None, None, None),
            P(),
        ),
        check_vma=False,
    )
```

```python
import math

import jax
import jax.numpy as jnp
import ml_dtypes
import numpy as np
from jax import lax
from jax.experimental import pallas as pl
from jax.experimental.pallas import tpu as pltpu
from jax.sharding import PartitionSpec as P

NX = 512
NY = 512
MODES = 16
CHAN = 32
FIELDS = 4
LAYERS = 2
GROUPS = 4
PER_GROUP = CHAN // GROUPS
ROWS = 32
KX = 2 * MODES
CELLS = NX * NY

highest = lax.Precision.HIGHEST
split = lax.Precision.HIGH
courant = 0.08
damage_rate = 0.5
strain_limit = 1.0
borehole_attenuation = 0.95
F32 = jnp.float32
BF16 = jnp.bfloat16
NN = (((1,), (0,)), ((), ()))
NT = (((1,), (1,)), ((), ()))
TN = (((0,), (0,)), ((), ()))
GELU_A = math.sqrt(2.0 / math.pi)
GELU_B = 0.044715
VMEM_LIMIT = 40 * 1024 * 1024
STORE = 15
SLOPE, ACT, MIXED, GRAD, BACK = range(5)


def parts_of(table, count):
    parts = []
    for _ in range(count):
        part = table.astype(ml_dtypes.bfloat16)
        parts.append(part)
        table = table - part.astype(np.float64)
    return parts


def wave_tables():
    ky = np.arange(MODES)
    angle_y = 2.0 * np.pi / NY * (ky[:, None] * np.arange(NY)[None, :] % NY)
    along_y = np.concatenate([np.cos(angle_y), -np.sin(angle_y)], 0)
    kx = np.concatenate([np.arange(MODES), NX - MODES + np.arange(MODES)])
    angle_x = 2.0 * np.pi / NX * (np.arange(NX)[:, None] * kx[None, :] % NX)
    y1, y2, y3 = parts_of(along_y, 3)
    forward_y = np.concatenate([y1, y2, y3], 0)
    inverse_y = np.concatenate([y1, y1, y2], 0)
    c1, c2 = parts_of(np.cos(angle_x), 2)
    s1, s2 = parts_of(np.sin(angle_x), 2)
    return forward_y, inverse_y, np.stack([c1, s1, c2, s2], 0)


def block_tables(along_x):
    local = lax.dynamic_slice_in_dim(along_x, lax.axis_index("gx") * ROWS, ROWS, 1)
    eye = jnp.eye(PER_GROUP, dtype=BF16)
    wide = eye[:, None, None, :, None] * jnp.transpose(local, (1, 0, 2))[None, :, :, None, :]
    return wide.reshape(PER_GROUP * ROWS, 4 * PER_GROUP * KX)


def halves(value):
    high = value.astype(BF16)
    return high, (value - high.astype(F32)).astype(BF16)


def dot(left, right, dims):
    return lax.dot_general(left, right, dims, preferred_element_type=F32)


def along_y(cells, forward_y):
    high, low = halves(cells)
    first = dot(forward_y[...], high, NT)
    second = dot(forward_y[: 4 * MODES, :], low, NT)
    return first[: 2 * MODES] + (
        first[2 * MODES : 4 * MODES]
        + first[4 * MODES :]
        + second[: 2 * MODES]
        + second[2 * MODES :]
    )


def along_x(pieces, blocks, dims, width):
    count = len(pieces)
    rows = 2 * MODES * count
    stacked = jnp.concatenate(halves(jnp.concatenate(pieces, 0)), 0)
    span = PER_GROUP * KX
    table = [blocks[:width, k * span : k * span + width] for k in range(4)]
    cos_1, sin_1 = [dot(stacked, part, dims) for part in table[:2]]
    cos_2, sin_2 = [dot(stacked[:rows], part, dims) for part in table[2:]]
    cos = cos_1[:rows] + (cos_1[rows:] + cos_2)
    sin = sin_1[:rows] + (sin_1[rows:] + sin_2)
    cut = [slice(2 * MODES * k, 2 * MODES * (k + 1)) for k in range(count)]
    return [(cos[at], sin[at]) for at in cut]


def forward_x(pieces, blocks, width):
    return [
        (cos[:MODES] + sin[MODES:], cos[MODES:] - sin[:MODES])
        for cos, sin in along_x(pieces, blocks, NN, width)
    ]


def inverse_x(modes, scaled, blocks, held):
    pieces = []
    for g in range(GROUPS):
        real = jnp.concatenate([modes[:, 2 * g, :], modes[:, 2 * g + 1, :]], 1)
        imag = jnp.concatenate([modes[:, 8 + 2 * g, :], modes[:, 9 + 2 * g, :]], 1)
        pieces.append(jnp.concatenate([scaled(real), scaled(imag)], 0))
    for g, (cos, sin) in enumerate(along_x(pieces, blocks, NT, PER_GROUP * ROWS)):
        rows = jnp.concatenate([cos[:MODES] - sin[MODES:], cos[MODES:] + sin[:MODES]], 0)
        high, low = halves(rows)
        held[g] = jnp.concatenate([high, low, high], 0)


def write_modes(sums, blocks, out):
    pieces = [sums[g] for g in range(GROUPS)]
    for g, (real, imag) in enumerate(forward_x(pieces, blocks, PER_GROUP * ROWS)):
        out[:, 2 * g, :] = real[:, :128]
        out[:, 2 * g + 1, :] = real[:, 128:]
        out[:, 8 + 2 * g, :] = imag[:, :128]
        out[:, 9 + 2 * g, :] = imag[:, 128:]


def doubled(value):
    row = lax.broadcasted_iota(jnp.int32, value.shape, 0)
    return jnp.where(row == 0, value, 2.0 * value)


def gelu_terms(value):
    square = value * value
    bend = jnp.tanh(value * (GELU_A + (GELU_A * GELU_B) * square))
    half = 0.5 + 0.5 * bend
    slope = half + (value * (1.0 - bend * bend)) * (0.5 * GELU_A + (1.5 * GELU_A * GELU_B) * square)
    return value * half, slope


def before_kernel(place, stiff, position, charge, now, prior, fracture, region, base, stiffness):
    zones = region[...]
    modulus = jnp.zeros(zones.shape, F32)
    for k in range(stiff.shape[0]):
        modulus = jnp.where(zones == k, stiff[k], modulus)
    stiffness[...] = modulus * (1.0 - fracture[...])
    depth, rows, _ = now.shape
    cell = (
        (place[0] * depth + lax.broadcasted_iota(jnp.int32, now.shape, 0)) * CELLS
        + (place[1] * rows + lax.broadcasted_iota(jnp.int32, now.shape, 1)) * NY
        + lax.broadcasted_iota(jnp.int32, now.shape, 2)
    )
    source = jnp.zeros(now.shape, F32)
    for h in range(position.shape[0]):
        source = source + jnp.where(cell == position[h], charge[h], 0.0)
    base[...] = 2.0 * now[...] - prior[...] + source


def solver_kernel(place, now, over, above, below, base, stiffness, fracture, ahead, damage, fields, wide):
    depth, rows, _ = now.shape
    wide[...] = jnp.zeros(wide.shape, F32)
    wide[:, 1:2, :] = above[...]
    wide[:, 2 : 2 + rows, :] = now[...]
    wide[:, 2 + rows : 3 + rows, :] = below[...]
    upper = place[0] == 1
    lane = lax.broadcasted_iota(jnp.int32, (rows, NY), 1)
    for z in range(depth):
        here = now[z]
        other = over[0]
        before_z = now[z - 1] if z > 0 else jnp.where(upper, other, 0.0)
        after_z = now[z + 1] if z < depth - 1 else jnp.where(upper, 0.0, other)
        before_x = wide[z, 1 : 1 + rows, :]
        after_x = wide[z, 3 : 3 + rows, :]
        before_y = jnp.where(lane == 0, 0.0, pltpu.roll(here, 1, 1))
        after_y = jnp.where(lane == NY - 1, 0.0, pltpu.roll(here, NY - 1, 1))
        laplace = after_z + before_z + after_x + before_x + after_y + before_y - 6.0 * here
        strain_z = 0.5 * (after_z - before_z)
        strain_x = 0.5 * (after_x - before_x)
        strain_y = 0.5 * (after_y - before_y)
        stiff = stiffness[z]
        moved = base[z] + courant * stiff * laplace
        square = strain_x * strain_x + strain_y * strain_y + strain_z * strain_z
        broken = fracture[z]
        grown = broken + (1.0 - broken) * jnp.tanh(
            damage_rate * jnp.maximum(square - strain_limit, 0.0)
        )
        ahead[z] = moved
        damage[z] = grown
        fields[z, 0] = moved
        fields[z, 1] = grown
        fields[z, 2] = stiff * strain_x
        fields[z, 3] = stiff * strain_y


def field_kernel(landed, forward_y, blocks, fields, out):
    blocks_in, _, rows, _ = landed.shape
    for k in range(blocks_in):
        for f in range(FIELDS):
            fields[f, k * rows : (k + 1) * rows, :] = landed[k, f]
    sums = along_y(fields[...].reshape(FIELDS * ROWS, NY), forward_y)
    ((real, imag),) = forward_x([sums], blocks, FIELDS * ROWS)
    for k in range(out.shape[0]):
        out[k, :MODES, :] = real * (1.0 / CELLS)
        out[k, MODES:, :] = imag * (1.0 / CELLS)


def sum_of(landed):
    parts = [landed[k] for k in range(landed.shape[0])]
    while len(parts) > 1:
        parts = [left + right for left, right in zip(parts[::2], parts[1::2])]
    return parts[0]


def lift_kernel(place, landed, own, other, spread, sums, out):
    total = sum_of(landed)
    sums[...] = total
    wide = exact(total, spread[...], NN)
    upper = place[0] == 1
    lane = lax.broadcasted_iota(jnp.int32, (MODES, 8, 128), 2)
    first = lax.broadcasted_iota(jnp.int32, (MODES, 8, 128), 0)
    shift = jnp.where(upper, other[:, 1], own[:, 1])
    real = jnp.where((first == 0) & (lane % KX == 0), shift, 0.0)
    imag = jnp.zeros((MODES, 8, 128), F32)
    for f in range(FIELDS):
        k = 2 * (f % 2)
        near = upper if f >= 2 else jnp.logical_not(upper)
        weight_re = jnp.where(near, own[:, k], other[:, k])
        weight_im = jnp.where(near, own[:, k + 1], other[:, k + 1])
        one_re = wide[:MODES, f * 128 : (f + 1) * 128][:, None, :]
        one_im = wide[MODES:, f * 128 : (f + 1) * 128][:, None, :]
        real = real + (one_re * weight_re - one_im * weight_im)
        imag = imag + (one_re * weight_im + one_im * weight_re)
    out[:, 0:8, :] = real
    out[:, 8:16, :] = imag


def by_kx(total, order):
    turned = total.T
    rows = jnp.zeros((KX, 2 * CHAN), F32)
    for f in range(4):
        rows = rows + lax.dot_general(
            turned[f * KX : (f + 1) * KX], order[f], NN, precision=highest, preferred_element_type=F32
        )
    return jnp.concatenate([rows[:MODES], rows[MODES:]], 1)


def apply_weights(adjoint, total, weights, spread, order, sums, out):
    wide = exact(total, spread[...], NN)
    real = jnp.zeros((8, 128), F32)
    imag = jnp.zeros((8, 128), F32)
    for i in range(CHAN):
        at, f = i // 4, i % 4
        one_re = wide[at : at + 1, f * 128 : (f + 1) * 128]
        one_im = wide[8 + at : 9 + at, f * 128 : (f + 1) * 128]
        weight_re = weights[i, 0]
        weight_im = weights[i, 1]
        if adjoint:
            real = real + (one_re * weight_re + one_im * weight_im)
            imag = imag + (one_im * weight_re - one_re * weight_im)
        else:
            real = real + (one_re * weight_re - one_im * weight_im)
            imag = imag + (one_re * weight_im + one_im * weight_re)
    for k in range(out.shape[0]):
        out[k, 0:8, :] = real
        out[k, 8:16, :] = imag
    sums[...] = by_kx(total, order)


def owner_kernel(adjoint, scale, landed, weights, spread, order, sums, out):
    total = sum_of(landed) * scale[0]
    apply_weights(adjoint, total, weights, spread, order, sums, out)


def group_of(ref, g):
    return ref.at[g * PER_GROUP : (g + 1) * PER_GROUP]


def part_of(ref, part):
    return ref.at[:, part * 8 : part * 8 + 8, :]


def copies(source, target, sems, cut):
    return [pltpu.make_async_copy(cut(source, k), cut(target, k), sems.at[k]) for k in range(GROUPS)]


def first_kernel(
    modes, fields, field_mix, field_shift, forward_y, inverse_y, blocks, store, out, held, sums, slope, act, sems
):
    leaving = copies(slope, store.at[SLOPE], sems.at[0], group_of)
    beside = copies(act, store.at[ACT], sems.at[1], group_of)
    inverse_x(modes, doubled, blocks, held)
    for g in range(GROUPS):
        pre = dot(held[g], inverse_y[...], TN).reshape(PER_GROUP, ROWS, NY)
        for k in range(PER_GROUP):
            c = g * PER_GROUP + k
            value = pre[k] + field_shift[c]
            for f in range(FIELDS):
                value = value + field_mix[f, c] * fields[f]
            act[c], slope[c] = gelu_terms(value)
        leaving[g].start()
        beside[g].start()
        cells = act[g * PER_GROUP : (g + 1) * PER_GROUP].reshape(PER_GROUP * ROWS, NY)
        sums[g] = along_y(cells, forward_y)
    write_modes(sums, blocks, out)
    for copy in leaving + beside:
        copy.wait()


def second_kernel(
    modes, store_in, sensitivity, decoder, forward_y, inverse_y, blocks, store, out, held, sums, mixed, grad, sems
):
    coming = copies(store.at[MIXED], mixed, sems.at[0], group_of)
    leaving = copies(grad, store.at[GRAD], sems.at[1], group_of)
    for copy in coming:
        copy.start()
    inverse_x(modes, doubled, blocks, held)
    for g in range(GROUPS):
        pre = dot(held[g], inverse_y[...], TN).reshape(PER_GROUP, ROWS, NY)
        coming[g].wait()
        for k in range(PER_GROUP):
            c = g * PER_GROUP + k
            _, slope = gelu_terms(pre[k] + mixed[c])
            grad[c] = slope * (decoder[c] * sensitivity[...])
        leaving[g].start()
        cells = grad[g * PER_GROUP : (g + 1) * PER_GROUP].reshape(PER_GROUP * ROWS, NY)
        sums[g] = along_y(cells, forward_y)
    write_modes(sums, blocks, out)
    for copy in leaving:
        copy.wait()


def back_kernel(
    modes, store, fields, pairs, forward_y, inverse_y, blocks, out, held, sums, mixed, slope, cells, sems
):
    coming = copies(store.at[BACK], mixed, sems.at[0], group_of)
    beside = copies(store.at[SLOPE], slope, sems.at[1], group_of)
    for g in range(GROUPS):
        coming[g].start()
        beside[g].start()
    inverse_x(modes, lambda value: value * (1.0 / CELLS), blocks, held)
    lane = lax.broadcasted_iota(jnp.int32, (8, 128), 1)
    dots = jnp.zeros((8, 128), F32)
    for g in range(GROUPS):
        pre = dot(held[g], inverse_y[...], TN).reshape(PER_GROUP, ROWS, NY)
        coming[g].wait()
        beside[g].wait()
        for k in range(PER_GROUP):
            c = g * PER_GROUP + k
            value = (pre[k] + mixed[c]) * slope[c]
            cells[g % 2, k] = value
            lines = []
            for f in range(FIELDS + 1):
                term = value if f == FIELDS else value * fields[f]
                term = (term[:, 0:128] + term[:, 128:256]) + (term[:, 256:384] + term[:, 384:512])
                term = (term[0:8] + term[8:16]) + (term[16:24] + term[24:32])
                lines.append(jnp.sum(term, axis=0, keepdims=True))
            lines.append(jnp.zeros((7 - FIELDS, 128), F32))
            total = jnp.sum(jnp.concatenate(lines, 0), axis=1, keepdims=True)
            dots = jnp.where(lane == c, total, dots)
        sums[g] = along_y(cells[g % 2].reshape(PER_GROUP * ROWS, NY), forward_y)
    write_modes(sums, blocks, out)
    for k in range(out.shape[0]):
        out[k, 16:24, :] = pairs[...]
        out[k, 24:32, :] = dots


def picker():
    row = lax.broadcasted_iota(jnp.int32, (CHAN * 8, CHAN), 0)
    column = lax.broadcasted_iota(jnp.int32, (CHAN * 8, CHAN), 1)
    return jnp.where(row // 8 == column, 1.0, 0.0).astype(F32)


def same_row(value):
    row = lax.broadcasted_iota(jnp.int32, value.shape, 0)
    column = lax.broadcasted_iota(jnp.int32, value.shape, 1)
    return jnp.where(row % 8 == column % 8, value, 0.0)


def exact(left, right, dims):
    return lax.dot_general(left, right, dims, precision=highest, preferred_element_type=F32)


def mix_rows(cells, high_m, low_m, part):
    cells = cells[:, part * 8 : part * 8 + 8, :].reshape(CHAN * 8, NY)
    high, low = halves(cells)
    return high, low, dot(high_m, high, NN) + (dot(low_m, high, NN) + dot(high_m, low, NN))


def mix_kernel(store_in, matrix, shift, store, act, mixed, sems):
    coming = copies(store.at[ACT], act, sems.at[0], part_of)
    leaving = copies(mixed, store.at[MIXED], sems.at[1], part_of)
    for copy in coming:
        copy.start()
    pick = picker()
    high_m, low_m = halves(same_row(exact(exact(pick, matrix[...], NT), pick, NT)))
    for part in range(ROWS // 8):
        coming[part].wait()
        _, _, sums = mix_rows(act, high_m, low_m, part)
        sums = sums.reshape(CHAN, 8, NY)
        for c in range(CHAN):
            mixed[c, part * 8 : part * 8 + 8, :] = sums[c] + shift[c]
        leaving[part].start()
    for copy in leaving:
        copy.wait()


def mix_back_kernel(store_in, matrix, store, pairs, grad, act, mixed, sems):
    coming = copies(store.at[GRAD], grad, sems.at[0], part_of)
    leaving = copies(mixed, store.at[BACK], sems.at[1], part_of)
    beside = copies(store.at[ACT], act, sems.at[2], part_of)
    for part in range(GROUPS):
        coming[part].start()
        beside[part].start()
    pick = picker()
    high_m, low_m = halves(same_row(exact(exact(pick, matrix[...], NN), pick, NT)))
    total = jnp.zeros((CHAN * 8, CHAN * 8), F32)
    for part in range(ROWS // 8):
        coming[part].wait()
        grad_high, grad_low, sums = mix_rows(grad, high_m, low_m, part)
        mixed[:, part * 8 : part * 8 + 8, :] = sums.reshape(CHAN, 8, NY)
        leaving[part].start()
        beside[part].wait()
        act_high, act_low = halves(act[:, part * 8 : part * 8 + 8, :].reshape(CHAN * 8, NY))
        total = total + (
            dot(act_high, grad_high, NT) + (dot(act_low, grad_high, NT) + dot(act_high, grad_low, NT))
        )
    total = exact(exact(pick, same_row(total), TN), pick, NN)
    pairs[...] = jnp.concatenate([total[8 * k : 8 * k + 8] for k in range(4)], 1)
    for copy in leaving:
        copy.wait()


def message_kernel(scale, landed, order, out):
    total = sum_of(landed)
    out[0:16, :] = by_kx(total[0:16] * scale[0], order)
    out[16:32, :] = total[16:32]


def gradient_kernel(place, early_near, early_far, held, other, lift, spec, mix, early, late):
    near = held.shape[0]
    for k in range(near):
        early[k ^ place[0]] = early_near[k]
        early[(k + near) ^ place[0]] = early_far[k]
        late[k ^ place[0]] = held[k]
        late[(k + near) ^ place[0]] = other[k]
    for layer, (at_in, at_out) in enumerate(((early, late), (early, early))):
        first = MODES * layer
        second = 2 * MODES * layer
        left = jnp.transpose(at_in[:, first : first + MODES, :], (1, 0, 2)).reshape(16 * MODES, 128)
        right = jnp.transpose(at_out[:, second : second + MODES, :], (1, 0, 2)).reshape(16 * MODES, 128)
        turned = [right] + [pltpu.roll(right, 128 - CHAN * j, 1) for j in (1, 2, 3)]
        turned = [halves(value) for value in turned]
        high_l, low_l = halves(left)
        for k in range(MODES):
            at = slice(16 * k, 16 * k + 16)
            stacked = jnp.concatenate([high_l[at], low_l[at], high_l[at]], 0)
            quarters = [
                dot(stacked, jnp.concatenate([high[at], high[at], low[at]], 0), TN)
                for high, low in turned
            ]
            for half in range(2):
                row = half * 2 * CHAN
                real, imag = quarters[2 * half], quarters[2 * half + 1]
                middle, end = row + CHAN, row + 2 * CHAN
                kx = half * MODES + k
                spec[layer, 0, kx, 0] = real[row:middle, :CHAN] + imag[middle:end, :CHAN]
                spec[layer, 0, kx, 1] = imag[row:middle, :CHAN] - real[middle:end, :CHAN]
    total = late[0, 16:32, :]
    for k in range(1, 2 * near):
        total = total + late[k, 16:32, :]
    scale = 1.0 / math.sqrt(CELLS)
    mix[0] = exact(lift[...], total[8:16, :CHAN], TN) * scale
    for k in range(4):
        mix[1, 8 * k : 8 * k + 8, :] = total[0:8, CHAN * k : CHAN * (k + 1)] * scale


SCALARS = pl.BlockSpec(memory_space=pltpu.SMEM)
MODE_SHAPE = jax.ShapeDtypeStruct((MODES, 16, 128), F32)
STORE_SHAPE = jax.ShapeDtypeStruct((STORE, CHAN, ROWS, NY), F32)
CELLS_VMEM = pltpu.VMEM((CHAN, ROWS, NY), F32)
LAYER_SCRATCH = (
    pltpu.VMEM((GROUPS, 6 * MODES, PER_GROUP * ROWS), BF16),
    pltpu.VMEM((GROUPS, 2 * MODES, PER_GROUP * ROWS), F32),
)


def local_call(kernel, name, out_shape, scalar_args=(), count=0, flops=10**6, scratch=(), far_args=(), far_outs=()):
    vmem = pl.BlockSpec(memory_space=pltpu.VMEM)
    far = pl.BlockSpec(memory_space=pltpu.HBM)
    single = not isinstance(out_shape, tuple)
    outs = [far if k in far_outs else vmem for k in range(1 if single else len(out_shape))]
    return pl.pallas_call(
        kernel,
        name=name,
        in_specs=[
            SCALARS if k in scalar_args else far if k in far_args else vmem for k in range(count)
        ],
        out_specs=outs[0] if single else outs,
        out_shape=out_shape,
        scratch_shapes=scratch,
        input_output_aliases={k: j for k in far_args for j in far_outs},
        compiler_params=pltpu.CompilerParams(vmem_limit_bytes=VMEM_LIMIT),
        cost_estimate=pl.CostEstimate(flops=flops, bytes_accessed=4 * 2**20, transcendentals=0),
    )


def sum_blocks(rows, axis):
    return lax.all_to_all(rows, axis, split_axis=0, concat_axis=0, tiled=True)


def all_copies(block, count):
    return jnp.broadcast_to(block[None], (count,) + block.shape)


def gather_planes(block):
    held = block[None]
    for axis, bit in (("gy", 4), ("gy", 2), ("gy", 1)):
        count = lax.axis_size(axis)
        other = lax.ppermute(held, axis, [(i, i ^ bit) for i in range(count)])
        held = jnp.concatenate([held, other], 0)
    return held, lax.ppermute(held, "grp", [(0, 1), (1, 0)])


def shards(
    present_displacement,
    prior_displacement,
    fracture_state,
    grid_material_region,
    region_young_stiffness,
    borehole_grid_position,
    detonation_order,
    explosive_mass,
    output_loss_sensitivity,
    encoder_matrix,
    encoder_offset,
    fourier_mode_kernel,
    local_mixing_matrix,
    local_mixing_offset,
    decoder_matrix,
):
    depth, local_x, _ = present_displacement.shape
    at_x, at_z = lax.axis_index("gx"), lax.axis_index("grp")
    place = jnp.stack([at_z, lax.axis_index(("gx", "gy"))]).astype(jnp.int32)
    edge = jnp.where(at_z == 0, present_displacement[depth - 1 :], present_displacement[:1])
    over = lax.ppermute(edge, "grp", [(0, 1), (1, 0)])
    along = ("gx", "gy")
    ends = lax.axis_size(along) - 1
    above = lax.ppermute(present_displacement[:, local_x - 1 :], along, [(i, i + 1) for i in range(ends)])
    below = lax.ppermute(present_displacement[:, :1], along, [(i + 1, i) for i in range(ends)])
    charge = explosive_mass * jnp.power(borehole_attenuation, detonation_order.astype(F32))
    block_shape = jax.ShapeDtypeStruct(present_displacement.shape, F32)
    base, stiffness = local_call(
        before_kernel, "before", (block_shape, block_shape), scalar_args=(0, 1, 2, 3), count=8
    )(
        place,
        region_young_stiffness,
        borehole_grid_position,
        charge,
        present_displacement,
        prior_displacement,
        fracture_state,
        grid_material_region,
    )
    advanced_displacement, advanced_fracture_state, message = local_call(
        solver_kernel,
        "solver",
        (block_shape, block_shape, jax.ShapeDtypeStruct((depth, FIELDS, local_x, NY), F32)),
        scalar_args=(0,),
        count=8,
        scratch=(pltpu.VMEM((depth, 8, NY), F32),),
    )(place, present_displacement, over, above, below, base, stiffness, fracture_state)
    weights_0 = fourier_mode_kernel[0, 0]
    at_mean = (jnp.arange(KX) == 0) & (at_x == 0)
    matrix = jnp.concatenate([encoder_matrix, encoder_offset[None]], 0)
    lifted = jnp.einsum("fi,krio->frok", matrix, weights_0, precision=highest)
    slot = (jnp.arange(FIELDS * 2) == 1).reshape(FIELDS, 2, 1, 1) & at_mean
    lifted = jnp.where(slot, lifted[FIELDS, 0], lifted[:FIELDS])
    lifted = lifted.reshape(2, FIELDS, 8, 128)
    lifted = jnp.where(at_z == 0, lifted[0], lifted[1])
    lifted = sum_blocks(all_copies(lifted, MODES), "gx")
    message, lifted = lax.optimization_barrier((message, lifted))
    landed = lax.all_to_all(message, "gy", split_axis=0, concat_axis=0, tiled=True)
    lifted_other = lax.ppermute(lifted, "grp", [(0, 1), (1, 0)])

    table_fy, table_iy, table_x = wave_tables()
    forward_y = jnp.asarray(table_fy)
    inverse_y = jnp.asarray(table_iy)
    blocks = block_tables(jnp.asarray(table_x))
    spread = np.zeros((128, FIELDS, 4, KX), np.float32)
    for f in range(4):
        for k in range(KX):
            spread[f * KX + k, f, :, k] = 1.0
    spread = jnp.asarray(spread.reshape(128, 512))
    order = np.zeros((4, 2, 8, 2, 8, 4), np.float32)
    for f in range(4):
        for k in range(8):
            for part in range(2):
                order[f, part, k, part, k, f] = 1.0
    order = jnp.asarray(order.reshape(4, 16, 64))
    weights_1 = fourier_mode_kernel[1, 0]
    by_input = jnp.transpose(weights_1, (2, 1, 3, 0)).reshape(CHAN, 2, 8, 128)
    by_output = jnp.transpose(weights_1, (3, 1, 2, 0)).reshape(CHAN, 2, 8, 128)
    mix_0, mix_1 = local_mixing_matrix[0], local_mixing_matrix[1]
    field_mix = jnp.dot(encoder_matrix, mix_0, precision=highest)
    field_shift = jnp.dot(encoder_offset, mix_0, precision=highest) + local_mixing_offset[0]

    fields, field_modes = local_call(
        field_kernel,
        "fields",
        (
            jax.ShapeDtypeStruct((FIELDS, ROWS, NY), F32),
            jax.ShapeDtypeStruct((MODES, 2 * MODES, 128), F32),
        ),
        count=3,
    )(landed, forward_y, blocks)
    landed = sum_blocks(field_modes, "gx")
    field_sums, modes = local_call(
        lift_kernel,
        "lift",
        (jax.ShapeDtypeStruct((2 * MODES, 128), F32), MODE_SHAPE),
        scalar_args=(0,),
        count=5,
    )(place, landed, lifted, lifted_other, spread)
    store, partial = local_call(
        first_kernel,
        "first",
        (STORE_SHAPE, MODE_SHAPE),
        scalar_args=(2, 3),
        count=7,
        flops=2 * 10**9,
        scratch=LAYER_SCRATCH + (CELLS_VMEM, CELLS_VMEM, pltpu.SemaphoreType.DMA((2, GROUPS))),
        far_outs=(0,),
    )(modes, fields, field_mix, field_shift, forward_y, inverse_y, blocks)

    owner_shapes = (jax.ShapeDtypeStruct((16, 128), F32), MODE_SHAPE)
    m_ky = jnp.where(at_x == 0, 1.0, 2.0).astype(F32)[None]

    def owner(adjoint, landed, weights):
        def kernel(*refs):
            owner_kernel(adjoint, *refs)

        name = "owner_back" if adjoint else "owner"
        scale = m_ky if adjoint else jnp.full((1,), 1.0 / CELLS, F32)
        sums, out = local_call(kernel, name, owner_shapes, scalar_args=(0,), count=5)(
            scale, landed, weights, spread, order
        )
        return sums, sum_blocks(out, "gx")

    landed = sum_blocks(partial, "gx")
    store = local_call(
        mix_kernel,
        "mix",
        STORE_SHAPE,
        scalar_args=(2,),
        count=3,
        flops=10**9,
        scratch=(CELLS_VMEM, CELLS_VMEM, pltpu.SemaphoreType.DMA((2, GROUPS))),
        far_args=(0,),
        far_outs=(0,),
    )(store, mix_1, local_mixing_offset[1])
    modes_1, modes = owner(False, landed, by_input)
    store, partial = local_call(
        second_kernel,
        "second",
        (STORE_SHAPE, MODE_SHAPE),
        scalar_args=(3,),
        count=7,
        flops=2 * 10**9,
        scratch=LAYER_SCRATCH + (CELLS_VMEM, CELLS_VMEM, pltpu.SemaphoreType.DMA((2, GROUPS))),
        far_args=(1,),
        far_outs=(0,),
    )(modes, store, output_loss_sensitivity[0], decoder_matrix, forward_y, inverse_y, blocks)

    landed = sum_blocks(partial, "gx")
    store, pairs_1 = local_call(
        mix_back_kernel,
        "mix_back",
        (STORE_SHAPE, jax.ShapeDtypeStruct((8, 128), F32)),
        count=2,
        flops=2 * 10**9,
        scratch=(CELLS_VMEM, CELLS_VMEM, CELLS_VMEM, pltpu.SemaphoreType.DMA((3, GROUPS))),
        far_args=(0,),
        far_outs=(0,),
    )(store, mix_1)
    back_1, modes = owner(True, landed, by_output)
    partial = local_call(
        back_kernel,
        "back",
        jax.ShapeDtypeStruct((MODES, 32, 128), F32),
        count=7,
        flops=2 * 10**9,
        scratch=LAYER_SCRATCH
        + (CELLS_VMEM, CELLS_VMEM, pltpu.VMEM((2, PER_GROUP, ROWS, NY), F32), pltpu.SemaphoreType.DMA((2, GROUPS))),
        far_args=(1,),
    )(modes, store, fields, pairs_1, forward_y, inverse_y, blocks)

    landed = sum_blocks(partial, "gx")
    own_fields = lax.dynamic_slice_in_dim(field_sums.reshape(2, MODES, FIELDS, KX), at_x, 1, 1)[:, 0]
    modes_0 = jnp.einsum("rfk,fi->kri", own_fields, encoder_matrix, precision=highest)
    modes_0 = modes_0.at[:, 0].add(jnp.where(at_mean, 1.0, 0.0)[:, None] * encoder_offset[None, :])
    modes_0 = modes_0.reshape(2, MODES, 2 * CHAN)
    modes_0 = jnp.concatenate([modes_0[0], modes_0[1]], 1)
    early_near, early_far = gather_planes(jnp.concatenate([modes_0, modes_1, back_1], 0))
    message = local_call(
        message_kernel, "message", jax.ShapeDtypeStruct((32, 128), F32), scalar_args=(0,), count=3
    )(m_ky, landed, order)
    held, other = gather_planes(message)
    at_y = lax.axis_index("gy")
    slot = at_y // 4 + 2 * (at_y // 2 % 2) + 4 * (at_y % 2) + 8 * at_z
    lift = jnp.concatenate([encoder_matrix, encoder_offset[None], jnp.zeros((3, CHAN), F32)], 0)
    spec_grad, mix_grad = local_call(
        gradient_kernel,
        "gradients",
        (
            jax.ShapeDtypeStruct((LAYERS, 1, KX, 2, CHAN, CHAN), F32),
            jax.ShapeDtypeStruct((LAYERS, CHAN, CHAN), F32),
        ),
        scalar_args=(0,),
        count=6,
        scratch=(pltpu.VMEM((16, 48, 128), F32), pltpu.VMEM((16, 32, 128), F32)),
    )(slot.astype(jnp.int32)[None], early_near, early_far, held, other, lift)
    return advanced_displacement, advanced_fracture_state, spec_grad, mix_grad


def solution(mesh):
    return jax.shard_map(
        shards,
        mesh=mesh,
        in_specs=(
            P("grp", ("gx", "gy"), None),
            P("grp", ("gx", "gy"), None),
            P("grp", ("gx", "gy"), None),
            P("grp", ("gx", "gy"), None),
            P(),
            P(),
            P(),
            P(),
            P(("grp", "gy"), "gx", None),
            P(),
            P(),
            P(None, "gx", None, None, None, None),
            P(),
            P(),
            P(),
        ),
        out_specs=(
            P("grp", ("gx", "gy"), None),
            P("grp", ("gx", "gy"), None),
            P(None, "gx", None, None, None, None),
            P(),
        ),
        check_vma=False,
    )
```

```python
import math

import jax
import jax.numpy as jnp
import ml_dtypes
import numpy as np
from jax import lax
from jax.experimental import pallas as pl
from jax.experimental.pallas import tpu as pltpu
from jax.sharding import PartitionSpec as P

NX = 512
NY = 512
MODES = 16
CHAN = 32
FIELDS = 4
LAYERS = 2
GROUPS = 4
PER_GROUP = CHAN // GROUPS
ROWS = 32
KX = 2 * MODES
CELLS = NX * NY

highest = lax.Precision.HIGHEST
split = lax.Precision.HIGH
courant = 0.08
damage_rate = 0.5
strain_limit = 1.0
borehole_attenuation = 0.95
F32 = jnp.float32
BF16 = jnp.bfloat16
NN = (((1,), (0,)), ((), ()))
NT = (((1,), (1,)), ((), ()))
TN = (((0,), (0,)), ((), ()))
GELU_A = math.sqrt(2.0 / math.pi)
GELU_B = 0.044715
VMEM_LIMIT = 40 * 1024 * 1024
STORE = 15
SLOPE, ACT, MIXED, GRAD, BACK = range(5)


def parts_of(table, count):
    parts = []
    for _ in range(count):
        part = table.astype(ml_dtypes.bfloat16)
        parts.append(part)
        table = table - part.astype(np.float64)
    return parts


def wave_tables():
    ky = np.arange(MODES)
    angle_y = 2.0 * np.pi / NY * (ky[:, None] * np.arange(NY)[None, :] % NY)
    along_y = np.concatenate([np.cos(angle_y), -np.sin(angle_y)], 0)
    kx = np.concatenate([np.arange(MODES), NX - MODES + np.arange(MODES)])
    angle_x = 2.0 * np.pi / NX * (np.arange(NX)[:, None] * kx[None, :] % NX)
    y1, y2, y3 = parts_of(along_y, 3)
    forward_y = np.concatenate([y1, y2, y3], 0)
    inverse_y = np.concatenate([y1, y1, y2], 0)
    c1, c2 = parts_of(np.cos(angle_x), 2)
    s1, s2 = parts_of(np.sin(angle_x), 2)
    return forward_y, inverse_y, np.stack([c1, s1, c2, s2], 0)


def block_tables(along_x):
    local = lax.dynamic_slice_in_dim(along_x, lax.axis_index("gx") * ROWS, ROWS, 1)
    eye = jnp.eye(PER_GROUP, dtype=BF16)
    wide = eye[:, None, None, :, None] * jnp.transpose(local, (1, 0, 2))[None, :, :, None, :]
    return wide.reshape(PER_GROUP * ROWS, 4 * PER_GROUP * KX)


def halves(value):
    high = value.astype(BF16)
    return high, (value - high.astype(F32)).astype(BF16)


def dot(left, right, dims):
    return lax.dot_general(left, right, dims, preferred_element_type=F32)


def along_y(cells, forward_y):
    high, low = halves(cells)
    first = dot(forward_y[...], high, NT)
    second = dot(forward_y[: 4 * MODES, :], low, NT)
    return first[: 2 * MODES] + (
        first[2 * MODES : 4 * MODES]
        + first[4 * MODES :]
        + second[: 2 * MODES]
        + second[2 * MODES :]
    )


def along_x(pieces, blocks, dims, width):
    count = len(pieces)
    rows = 2 * MODES * count
    stacked = jnp.concatenate(halves(jnp.concatenate(pieces, 0)), 0)
    span = PER_GROUP * KX
    table = [blocks[:width, k * span : k * span + width] for k in range(4)]
    cos_1, sin_1 = [dot(stacked, part, dims) for part in table[:2]]
    cos_2, sin_2 = [dot(stacked[:rows], part, dims) for part in table[2:]]
    cos = cos_1[:rows] + (cos_1[rows:] + cos_2)
    sin = sin_1[:rows] + (sin_1[rows:] + sin_2)
    cut = [slice(2 * MODES * k, 2 * MODES * (k + 1)) for k in range(count)]
    return [(cos[at], sin[at]) for at in cut]


def forward_x(pieces, blocks, width):
    return [
        (cos[:MODES] + sin[MODES:], cos[MODES:] - sin[:MODES])
        for cos, sin in along_x(pieces, blocks, NN, width)
    ]


def inverse_x(modes, scaled, blocks, held):
    pieces = []
    for g in range(GROUPS):
        real = jnp.concatenate([modes[:, 2 * g, :], modes[:, 2 * g + 1, :]], 1)
        imag = jnp.concatenate([modes[:, 8 + 2 * g, :], modes[:, 9 + 2 * g, :]], 1)
        pieces.append(jnp.concatenate([scaled(real), scaled(imag)], 0))
    for g, (cos, sin) in enumerate(along_x(pieces, blocks, NT, PER_GROUP * ROWS)):
        rows = jnp.concatenate([cos[:MODES] - sin[MODES:], cos[MODES:] + sin[:MODES]], 0)
        high, low = halves(rows)
        held[g] = jnp.concatenate([high, low, high], 0)


def write_modes(sums, blocks, out):
    pieces = [sums[g] for g in range(GROUPS)]
    for g, (real, imag) in enumerate(forward_x(pieces, blocks, PER_GROUP * ROWS)):
        out[:, 2 * g, :] = real[:, :128]
        out[:, 2 * g + 1, :] = real[:, 128:]
        out[:, 8 + 2 * g, :] = imag[:, :128]
        out[:, 9 + 2 * g, :] = imag[:, 128:]


def doubled(value):
    row = lax.broadcasted_iota(jnp.int32, value.shape, 0)
    return jnp.where(row == 0, value, 2.0 * value)


def gelu_terms(value):
    square = value * value
    bend = jnp.tanh(value * (GELU_A + (GELU_A * GELU_B) * square))
    half = 0.5 + 0.5 * bend
    slope = half + (value * (1.0 - bend * bend)) * (0.5 * GELU_A + (1.5 * GELU_A * GELU_B) * square)
    return value * half, slope


def before_kernel(place, stiff, position, charge, now, prior, fracture, region, base, stiffness):
    zones = region[...]
    modulus = jnp.zeros(zones.shape, F32)
    for k in range(stiff.shape[0]):
        modulus = jnp.where(zones == k, stiff[k], modulus)
    stiffness[...] = modulus * (1.0 - fracture[...])
    depth, rows, _ = now.shape
    cell = (
        (place[0] * depth + lax.broadcasted_iota(jnp.int32, now.shape, 0)) * CELLS
        + (place[1] * rows + lax.broadcasted_iota(jnp.int32, now.shape, 1)) * NY
        + lax.broadcasted_iota(jnp.int32, now.shape, 2)
    )
    source = jnp.zeros(now.shape, F32)
    for h in range(position.shape[0]):
        source = source + jnp.where(cell == position[h], charge[h], 0.0)
    base[...] = 2.0 * now[...] - prior[...] + source


def solver_kernel(place, now, over, above, below, base, stiffness, fracture, ahead, damage, fields, wide):
    depth, rows, _ = now.shape
    wide[...] = jnp.zeros(wide.shape, F32)
    wide[:, 1:2, :] = above[...]
    wide[:, 2 : 2 + rows, :] = now[...]
    wide[:, 2 + rows : 3 + rows, :] = below[...]
    upper = place[0] == 1
    lane = lax.broadcasted_iota(jnp.int32, (rows, NY), 1)
    for z in range(depth):
        here = now[z]
        other = over[0]
        before_z = now[z - 1] if z > 0 else jnp.where(upper, other, 0.0)
        after_z = now[z + 1] if z < depth - 1 else jnp.where(upper, 0.0, other)
        before_x = wide[z, 1 : 1 + rows, :]
        after_x = wide[z, 3 : 3 + rows, :]
        before_y = jnp.where(lane == 0, 0.0, pltpu.roll(here, 1, 1))
        after_y = jnp.where(lane == NY - 1, 0.0, pltpu.roll(here, NY - 1, 1))
        laplace = after_z + before_z + after_x + before_x + after_y + before_y - 6.0 * here
        strain_z = 0.5 * (after_z - before_z)
        strain_x = 0.5 * (after_x - before_x)
        strain_y = 0.5 * (after_y - before_y)
        stiff = stiffness[z]
        moved = base[z] + courant * stiff * laplace
        square = strain_x * strain_x + strain_y * strain_y + strain_z * strain_z
        broken = fracture[z]
        grown = broken + (1.0 - broken) * jnp.tanh(
            damage_rate * jnp.maximum(square - strain_limit, 0.0)
        )
        ahead[z] = moved
        damage[z] = grown
        fields[z, 0] = moved
        fields[z, 1] = grown
        fields[z, 2] = stiff * strain_x
        fields[z, 3] = stiff * strain_y


def field_kernel(landed, forward_y, blocks, fields, out):
    blocks_in, _, rows, _ = landed.shape
    for k in range(blocks_in):
        for f in range(FIELDS):
            fields[f, k * rows : (k + 1) * rows, :] = landed[k, f]
    sums = along_y(fields[...].reshape(FIELDS * ROWS, NY), forward_y)
    ((real, imag),) = forward_x([sums], blocks, FIELDS * ROWS)
    for k in range(out.shape[0]):
        out[k, :MODES, :] = real * (1.0 / CELLS)
        out[k, MODES:, :] = imag * (1.0 / CELLS)


def sum_of(landed):
    parts = [landed[k] for k in range(landed.shape[0])]
    while len(parts) > 1:
        parts = [left + right for left, right in zip(parts[::2], parts[1::2])]
    return parts[0]


def lift_kernel(place, landed, own, other, spread, sums, out):
    total = sum_of(landed)
    sums[...] = total
    wide = exact(total, spread[...], NN)
    upper = place[0] == 1
    lane = lax.broadcasted_iota(jnp.int32, (MODES, 8, 128), 2)
    first = lax.broadcasted_iota(jnp.int32, (MODES, 8, 128), 0)
    shift = jnp.where(upper, other[:, 1], own[:, 1])
    real = jnp.where((first == 0) & (lane % KX == 0), shift, 0.0)
    imag = jnp.zeros((MODES, 8, 128), F32)
    for f in range(FIELDS):
        k = 2 * (f % 2)
        near = upper if f >= 2 else jnp.logical_not(upper)
        weight_re = jnp.where(near, own[:, k], other[:, k])
        weight_im = jnp.where(near, own[:, k + 1], other[:, k + 1])
        one_re = wide[:MODES, f * 128 : (f + 1) * 128][:, None, :]
        one_im = wide[MODES:, f * 128 : (f + 1) * 128][:, None, :]
        real = real + (one_re * weight_re - one_im * weight_im)
        imag = imag + (one_re * weight_im + one_im * weight_re)
    out[:, 0:8, :] = real
    out[:, 8:16, :] = imag


def by_kx(total, order):
    turned = total.T
    rows = jnp.zeros((KX, 2 * CHAN), F32)
    for f in range(4):
        rows = rows + lax.dot_general(
            turned[f * KX : (f + 1) * KX], order[f], NN, precision=highest, preferred_element_type=F32
        )
    return jnp.concatenate([rows[:MODES], rows[MODES:]], 1)


def apply_weights(adjoint, total, weights, spread, order, sums, out):
    wide = exact(total, spread[...], NN)
    real = jnp.zeros((8, 128), F32)
    imag = jnp.zeros((8, 128), F32)
    for i in range(CHAN):
        at, f = i // 4, i % 4
        one_re = wide[at : at + 1, f * 128 : (f + 1) * 128]
        one_im = wide[8 + at : 9 + at, f * 128 : (f + 1) * 128]
        weight_re = weights[i, 0]
        weight_im = weights[i, 1]
        if adjoint:
            real = real + (one_re * weight_re + one_im * weight_im)
            imag = imag + (one_im * weight_re - one_re * weight_im)
        else:
            real = real + (one_re * weight_re - one_im * weight_im)
            imag = imag + (one_re * weight_im + one_im * weight_re)
    for k in range(out.shape[0]):
        out[k, 0:8, :] = real
        out[k, 8:16, :] = imag
    sums[...] = by_kx(total, order)


def owner_kernel(adjoint, scale, landed, weights, spread, order, sums, out):
    total = sum_of(landed) * scale[0]
    apply_weights(adjoint, total, weights, spread, order, sums, out)


def group_of(ref, g):
    return ref.at[g * PER_GROUP : (g + 1) * PER_GROUP]


def part_of(ref, part):
    return ref.at[:, part * 8 : part * 8 + 8, :]


def copies(source, target, sems, cut):
    return [pltpu.make_async_copy(cut(source, k), cut(target, k), sems.at[k]) for k in range(GROUPS)]


def first_kernel(
    modes, fields, field_mix, field_shift, forward_y, inverse_y, blocks, store, out, held, sums, slope, act, sems
):
    leaving = copies(slope, store.at[SLOPE], sems.at[0], group_of)
    beside = copies(act, store.at[ACT], sems.at[1], group_of)
    inverse_x(modes, doubled, blocks, held)
    for g in range(GROUPS):
        pre = dot(held[g], inverse_y[...], TN).reshape(PER_GROUP, ROWS, NY)
        for k in range(PER_GROUP):
            c = g * PER_GROUP + k
            value = pre[k] + field_shift[c]
            for f in range(FIELDS):
                value = value + field_mix[f, c] * fields[f]
            act[c], slope[c] = gelu_terms(value)
        leaving[g].start()
        beside[g].start()
        cells = act[g * PER_GROUP : (g + 1) * PER_GROUP].reshape(PER_GROUP * ROWS, NY)
        sums[g] = along_y(cells, forward_y)
    write_modes(sums, blocks, out)
    for copy in leaving + beside:
        copy.wait()


def second_kernel(
    modes, store_in, sensitivity, decoder, forward_y, inverse_y, blocks, store, out, held, sums, mixed, grad, sems
):
    coming = copies(store.at[MIXED], mixed, sems.at[0], group_of)
    leaving = copies(grad, store.at[GRAD], sems.at[1], group_of)
    for copy in coming:
        copy.start()
    inverse_x(modes, doubled, blocks, held)
    for g in range(GROUPS):
        pre = dot(held[g], inverse_y[...], TN).reshape(PER_GROUP, ROWS, NY)
        coming[g].wait()
        for k in range(PER_GROUP):
            c = g * PER_GROUP + k
            _, slope = gelu_terms(pre[k] + mixed[c])
            grad[c] = slope * (decoder[c] * sensitivity[...])
        leaving[g].start()
        cells = grad[g * PER_GROUP : (g + 1) * PER_GROUP].reshape(PER_GROUP * ROWS, NY)
        sums[g] = along_y(cells, forward_y)
    write_modes(sums, blocks, out)
    for copy in leaving:
        copy.wait()


def back_kernel(
    modes, store, fields, pairs, forward_y, inverse_y, blocks, out, held, sums, mixed, slope, cells, sems
):
    coming = copies(store.at[BACK], mixed, sems.at[0], group_of)
    beside = copies(store.at[SLOPE], slope, sems.at[1], group_of)
    for g in range(GROUPS):
        coming[g].start()
        beside[g].start()
    inverse_x(modes, lambda value: value * (1.0 / CELLS), blocks, held)
    lane = lax.broadcasted_iota(jnp.int32, (8, 128), 1)
    dots = jnp.zeros((8, 128), F32)
    for g in range(GROUPS):
        pre = dot(held[g], inverse_y[...], TN).reshape(PER_GROUP, ROWS, NY)
        coming[g].wait()
        beside[g].wait()
        for k in range(PER_GROUP):
            c = g * PER_GROUP + k
            value = (pre[k] + mixed[c]) * slope[c]
            cells[g % 2, k] = value
            lines = []
            for f in range(FIELDS + 1):
                term = value if f == FIELDS else value * fields[f]
                term = (term[:, 0:128] + term[:, 128:256]) + (term[:, 256:384] + term[:, 384:512])
                term = (term[0:8] + term[8:16]) + (term[16:24] + term[24:32])
                lines.append(jnp.sum(term, axis=0, keepdims=True))
            lines.append(jnp.zeros((7 - FIELDS, 128), F32))
            total = jnp.sum(jnp.concatenate(lines, 0), axis=1, keepdims=True)
            dots = jnp.where(lane == c, total, dots)
        sums[g] = along_y(cells[g % 2].reshape(PER_GROUP * ROWS, NY), forward_y)
    write_modes(sums, blocks, out)
    for k in range(out.shape[0]):
        out[k, 16:24, :] = pairs[...]
        out[k, 24:32, :] = dots


def picker():
    row = lax.broadcasted_iota(jnp.int32, (CHAN * 8, CHAN), 0)
    column = lax.broadcasted_iota(jnp.int32, (CHAN * 8, CHAN), 1)
    return jnp.where(row // 8 == column, 1.0, 0.0).astype(F32)


def same_row(value):
    row = lax.broadcasted_iota(jnp.int32, value.shape, 0)
    column = lax.broadcasted_iota(jnp.int32, value.shape, 1)
    return jnp.where(row % 8 == column % 8, value, 0.0)


def exact(left, right, dims):
    return lax.dot_general(left, right, dims, precision=highest, preferred_element_type=F32)


def mix_rows(cells, high_m, low_m, part):
    cells = cells[:, part * 8 : part * 8 + 8, :].reshape(CHAN * 8, NY)
    high, low = halves(cells)
    return high, low, dot(high_m, high, NN) + (dot(low_m, high, NN) + dot(high_m, low, NN))


def mix_kernel(store_in, matrix, shift, store, act, mixed, sems):
    coming = copies(store.at[ACT], act, sems.at[0], part_of)
    leaving = copies(mixed, store.at[MIXED], sems.at[1], part_of)
    for copy in coming:
        copy.start()
    pick = picker()
    high_m, low_m = halves(same_row(exact(exact(pick, matrix[...], NT), pick, NT)))
    for part in range(ROWS // 8):
        coming[part].wait()
        _, _, sums = mix_rows(act, high_m, low_m, part)
        sums = sums.reshape(CHAN, 8, NY)
        for c in range(CHAN):
            mixed[c, part * 8 : part * 8 + 8, :] = sums[c] + shift[c]
        leaving[part].start()
    for copy in leaving:
        copy.wait()


def mix_back_kernel(store_in, matrix, store, pairs, grad, act, mixed, sems):
    coming = copies(store.at[GRAD], grad, sems.at[0], part_of)
    leaving = copies(mixed, store.at[BACK], sems.at[1], part_of)
    beside = copies(store.at[ACT], act, sems.at[2], part_of)
    for part in range(GROUPS):
        coming[part].start()
        beside[part].start()
    pick = picker()
    high_m, low_m = halves(same_row(exact(exact(pick, matrix[...], NN), pick, NT)))
    total = jnp.zeros((CHAN * 8, CHAN * 8), F32)
    for part in range(ROWS // 8):
        coming[part].wait()
        grad_high, grad_low, sums = mix_rows(grad, high_m, low_m, part)
        mixed[:, part * 8 : part * 8 + 8, :] = sums.reshape(CHAN, 8, NY)
        leaving[part].start()
        beside[part].wait()
        act_high, act_low = halves(act[:, part * 8 : part * 8 + 8, :].reshape(CHAN * 8, NY))
        total = total + (
            dot(act_high, grad_high, NT) + (dot(act_low, grad_high, NT) + dot(act_high, grad_low, NT))
        )
    total = exact(exact(pick, same_row(total), TN), pick, NN)
    pairs[...] = jnp.concatenate([total[8 * k : 8 * k + 8] for k in range(4)], 1)
    for copy in leaving:
        copy.wait()


def message_kernel(scale, landed, order, out):
    total = sum_of(landed)
    out[0:16, :] = by_kx(total[0:16] * scale[0], order)
    out[16:32, :] = total[16:32]


def spectral_gradient(at_in, first, at_out, second, spec):
    left = jnp.transpose(at_in[:, first : first + MODES, :], (1, 0, 2)).reshape(16 * MODES, 128)
    right = jnp.transpose(at_out[:, second : second + MODES, :], (1, 0, 2)).reshape(16 * MODES, 128)
    turned = [right] + [pltpu.roll(right, 128 - CHAN * j, 1) for j in (1, 2, 3)]
    turned = [halves(value) for value in turned]
    high_l, low_l = halves(left)
    for k in range(MODES):
        at = slice(16 * k, 16 * k + 16)
        stacked = jnp.concatenate([high_l[at], low_l[at], high_l[at]], 0)
        quarters = [
            dot(stacked, jnp.concatenate([high[at], high[at], low[at]], 0), TN)
            for high, low in turned
        ]
        for half in range(2):
            row = half * 2 * CHAN
            real, imag = quarters[2 * half], quarters[2 * half + 1]
            middle, end = row + CHAN, row + 2 * CHAN
            kx = half * MODES + k
            spec[kx, 0] = real[row:middle, :CHAN] + imag[middle:end, :CHAN]
            spec[kx, 1] = imag[row:middle, :CHAN] - real[middle:end, :CHAN]


def arranged(place, near, far, planes):
    count = near.shape[0]
    for k in range(count):
        planes[k ^ place[0]] = near[k]
        planes[(k + count) ^ place[0]] = far[k]


def early_kernel(place, near, far, out, early, spec, sem):
    arranged(place, near, far, early)
    spectral_gradient(early, MODES, early, 2 * MODES, spec)
    copy = pltpu.make_async_copy(spec, out.at[1, 0], sem)
    copy.start()
    copy.wait()


def gradient_kernel(place, begun, early_near, early_far, held, other, lift, out, mix, early, late, spec, sem):
    arranged(place, early_near, early_far, early)
    arranged(place, held, other, late)
    near = held.shape[0]
    spectral_gradient(early, 0, late, 0, spec)
    copy = pltpu.make_async_copy(spec, out.at[0, 0], sem)
    copy.start()
    total = late[0, 16:32, :]
    for k in range(1, 2 * near):
        total = total + late[k, 16:32, :]
    scale = 1.0 / math.sqrt(CELLS)
    mix[0] = exact(lift[...], total[8:16, :CHAN], TN) * scale
    for k in range(4):
        mix[1, 8 * k : 8 * k + 8, :] = total[0:8, CHAN * k : CHAN * (k + 1)] * scale
    copy.wait()


SCALARS = pl.BlockSpec(memory_space=pltpu.SMEM)
MODE_SHAPE = jax.ShapeDtypeStruct((MODES, 16, 128), F32)
STORE_SHAPE = jax.ShapeDtypeStruct((STORE, CHAN, ROWS, NY), F32)
CELLS_VMEM = pltpu.VMEM((CHAN, ROWS, NY), F32)
LAYER_SCRATCH = (
    pltpu.VMEM((GROUPS, 6 * MODES, PER_GROUP * ROWS), BF16),
    pltpu.VMEM((GROUPS, 2 * MODES, PER_GROUP * ROWS), F32),
)


def local_call(kernel, name, out_shape, scalar_args=(), count=0, flops=10**6, scratch=(), far_args=(), far_outs=()):
    vmem = pl.BlockSpec(memory_space=pltpu.VMEM)
    far = pl.BlockSpec(memory_space=pltpu.HBM)
    single = not isinstance(out_shape, tuple)
    outs = [far if k in far_outs else vmem for k in range(1 if single else len(out_shape))]
    return pl.pallas_call(
        kernel,
        name=name,
        in_specs=[
            SCALARS if k in scalar_args else far if k in far_args else vmem for k in range(count)
        ],
        out_specs=outs[0] if single else outs,
        out_shape=out_shape,
        scratch_shapes=scratch,
        input_output_aliases={k: j for k in far_args for j in far_outs},
        compiler_params=pltpu.CompilerParams(vmem_limit_bytes=VMEM_LIMIT),
        cost_estimate=pl.CostEstimate(flops=flops, bytes_accessed=4 * 2**20, transcendentals=0),
    )


def sum_blocks(rows, axis):
    return lax.all_to_all(rows, axis, split_axis=0, concat_axis=0, tiled=True)


def all_copies(block, count):
    return jnp.broadcast_to(block[None], (count,) + block.shape)


def gather_planes(block):
    held = block[None]
    for axis, bit in (("gy", 4), ("gy", 2), ("gy", 1)):
        count = lax.axis_size(axis)
        other = lax.ppermute(held, axis, [(i, i ^ bit) for i in range(count)])
        held = jnp.concatenate([held, other], 0)
    return held, lax.ppermute(held, "grp", [(0, 1), (1, 0)])


def shards(
    present_displacement,
    prior_displacement,
    fracture_state,
    grid_material_region,
    region_young_stiffness,
    borehole_grid_position,
    detonation_order,
    explosive_mass,
    output_loss_sensitivity,
    encoder_matrix,
    encoder_offset,
    fourier_mode_kernel,
    local_mixing_matrix,
    local_mixing_offset,
    decoder_matrix,
):
    depth, local_x, _ = present_displacement.shape
    at_x, at_z = lax.axis_index("gx"), lax.axis_index("grp")
    place = jnp.stack([at_z, lax.axis_index(("gx", "gy"))]).astype(jnp.int32)
    edge = jnp.where(at_z == 0, present_displacement[depth - 1 :], present_displacement[:1])
    over = lax.ppermute(edge, "grp", [(0, 1), (1, 0)])
    along = ("gx", "gy")
    ends = lax.axis_size(along) - 1
    above = lax.ppermute(present_displacement[:, local_x - 1 :], along, [(i, i + 1) for i in range(ends)])
    below = lax.ppermute(present_displacement[:, :1], along, [(i + 1, i) for i in range(ends)])
    charge = explosive_mass * jnp.power(borehole_attenuation, detonation_order.astype(F32))
    block_shape = jax.ShapeDtypeStruct(present_displacement.shape, F32)
    base, stiffness = local_call(
        before_kernel, "before", (block_shape, block_shape), scalar_args=(0, 1, 2, 3), count=8
    )(
        place,
        region_young_stiffness,
        borehole_grid_position,
        charge,
        present_displacement,
        prior_displacement,
        fracture_state,
        grid_material_region,
    )
    advanced_displacement, advanced_fracture_state, message = local_call(
        solver_kernel,
        "solver",
        (block_shape, block_shape, jax.ShapeDtypeStruct((depth, FIELDS, local_x, NY), F32)),
        scalar_args=(0,),
        count=8,
        scratch=(pltpu.VMEM((depth, 8, NY), F32),),
    )(place, present_displacement, over, above, below, base, stiffness, fracture_state)
    weights_0 = fourier_mode_kernel[0, 0]
    at_mean = (jnp.arange(KX) == 0) & (at_x == 0)
    matrix = jnp.concatenate([encoder_matrix, encoder_offset[None]], 0)
    lifted = jnp.einsum("fi,krio->frok", matrix, weights_0, precision=highest)
    slot = (jnp.arange(FIELDS * 2) == 1).reshape(FIELDS, 2, 1, 1) & at_mean
    lifted = jnp.where(slot, lifted[FIELDS, 0], lifted[:FIELDS])
    lifted = lifted.reshape(2, FIELDS, 8, 128)
    lifted = jnp.where(at_z == 0, lifted[0], lifted[1])
    lifted = sum_blocks(all_copies(lifted, MODES), "gx")
    message, lifted = lax.optimization_barrier((message, lifted))
    landed = lax.all_to_all(message, "gy", split_axis=0, concat_axis=0, tiled=True)
    lifted_other = lax.ppermute(lifted, "grp", [(0, 1), (1, 0)])

    table_fy, table_iy, table_x = wave_tables()
    forward_y = jnp.asarray(table_fy)
    inverse_y = jnp.asarray(table_iy)
    blocks = block_tables(jnp.asarray(table_x))
    spread = np.zeros((128, FIELDS, 4, KX), np.float32)
    for f in range(4):
        for k in range(KX):
            spread[f * KX + k, f, :, k] = 1.0
    spread = jnp.asarray(spread.reshape(128, 512))
    order = np.zeros((4, 2, 8, 2, 8, 4), np.float32)
    for f in range(4):
        for k in range(8):
            for part in range(2):
                order[f, part, k, part, k, f] = 1.0
    order = jnp.asarray(order.reshape(4, 16, 64))
    weights_1 = fourier_mode_kernel[1, 0]
    by_input = jnp.transpose(weights_1, (2, 1, 3, 0)).reshape(CHAN, 2, 8, 128)
    by_output = jnp.transpose(weights_1, (3, 1, 2, 0)).reshape(CHAN, 2, 8, 128)
    mix_0, mix_1 = local_mixing_matrix[0], local_mixing_matrix[1]
    field_mix = jnp.dot(encoder_matrix, mix_0, precision=highest)
    field_shift = jnp.dot(encoder_offset, mix_0, precision=highest) + local_mixing_offset[0]

    fields, field_modes = local_call(
        field_kernel,
        "fields",
        (
            jax.ShapeDtypeStruct((FIELDS, ROWS, NY), F32),
            jax.ShapeDtypeStruct((MODES, 2 * MODES, 128), F32),
        ),
        count=3,
    )(landed, forward_y, blocks)
    landed = sum_blocks(field_modes, "gx")
    field_sums, modes = local_call(
        lift_kernel,
        "lift",
        (jax.ShapeDtypeStruct((2 * MODES, 128), F32), MODE_SHAPE),
        scalar_args=(0,),
        count=5,
    )(place, landed, lifted, lifted_other, spread)
    store, partial = local_call(
        first_kernel,
        "first",
        (STORE_SHAPE, MODE_SHAPE),
        scalar_args=(2, 3),
        count=7,
        flops=2 * 10**9,
        scratch=LAYER_SCRATCH + (CELLS_VMEM, CELLS_VMEM, pltpu.SemaphoreType.DMA((2, GROUPS))),
        far_outs=(0,),
    )(modes, fields, field_mix, field_shift, forward_y, inverse_y, blocks)

    owner_shapes = (jax.ShapeDtypeStruct((16, 128), F32), MODE_SHAPE)
    m_ky = jnp.where(at_x == 0, 1.0, 2.0).astype(F32)[None]

    def owner(adjoint, landed, weights):
        def kernel(*refs):
            owner_kernel(adjoint, *refs)

        name = "owner_back" if adjoint else "owner"
        scale = m_ky if adjoint else jnp.full((1,), 1.0 / CELLS, F32)
        sums, out = local_call(kernel, name, owner_shapes, scalar_args=(0,), count=5)(
            scale, landed, weights, spread, order
        )
        return sums, sum_blocks(out, "gx")

    landed = sum_blocks(partial, "gx")
    store = local_call(
        mix_kernel,
        "mix",
        STORE_SHAPE,
        scalar_args=(2,),
        count=3,
        flops=10**9,
        scratch=(CELLS_VMEM, CELLS_VMEM, pltpu.SemaphoreType.DMA((2, GROUPS))),
        far_args=(0,),
        far_outs=(0,),
    )(store, mix_1, local_mixing_offset[1])
    modes_1, modes = owner(False, landed, by_input)
    store, partial = local_call(
        second_kernel,
        "second",
        (STORE_SHAPE, MODE_SHAPE),
        scalar_args=(3,),
        count=7,
        flops=2 * 10**9,
        scratch=LAYER_SCRATCH + (CELLS_VMEM, CELLS_VMEM, pltpu.SemaphoreType.DMA((2, GROUPS))),
        far_args=(1,),
        far_outs=(0,),
    )(modes, store, output_loss_sensitivity[0], decoder_matrix, forward_y, inverse_y, blocks)

    landed = sum_blocks(partial, "gx")
    store, pairs_1 = local_call(
        mix_back_kernel,
        "mix_back",
        (STORE_SHAPE, jax.ShapeDtypeStruct((8, 128), F32)),
        count=2,
        flops=2 * 10**9,
        scratch=(CELLS_VMEM, CELLS_VMEM, CELLS_VMEM, pltpu.SemaphoreType.DMA((3, GROUPS))),
        far_args=(0,),
        far_outs=(0,),
    )(store, mix_1)
    back_1, modes = owner(True, landed, by_output)
    partial = local_call(
        back_kernel,
        "back",
        jax.ShapeDtypeStruct((MODES, 32, 128), F32),
        count=7,
        flops=2 * 10**9,
        scratch=LAYER_SCRATCH
        + (CELLS_VMEM, CELLS_VMEM, pltpu.VMEM((2, PER_GROUP, ROWS, NY), F32), pltpu.SemaphoreType.DMA((2, GROUPS))),
        far_args=(1,),
    )(modes, store, fields, pairs_1, forward_y, inverse_y, blocks)

    landed = sum_blocks(partial, "gx")
    own_fields = lax.dynamic_slice_in_dim(field_sums.reshape(2, MODES, FIELDS, KX), at_x, 1, 1)[:, 0]
    modes_0 = jnp.einsum("rfk,fi->kri", own_fields, encoder_matrix, precision=highest)
    modes_0 = modes_0.at[:, 0].add(jnp.where(at_mean, 1.0, 0.0)[:, None] * encoder_offset[None, :])
    modes_0 = modes_0.reshape(2, MODES, 2 * CHAN)
    modes_0 = jnp.concatenate([modes_0[0], modes_0[1]], 1)
    early_near, early_far = gather_planes(jnp.concatenate([modes_0, modes_1, back_1], 0))
    message = local_call(
        message_kernel, "message", jax.ShapeDtypeStruct((32, 128), F32), scalar_args=(0,), count=3
    )(m_ky, landed, order)
    held, other = gather_planes(message)
    at_y = lax.axis_index("gy")
    slot = at_y // 4 + 2 * (at_y // 2 % 2) + 4 * (at_y % 2) + 8 * at_z
    lift = jnp.concatenate([encoder_matrix, encoder_offset[None], jnp.zeros((3, CHAN), F32)], 0)
    slot = slot.astype(jnp.int32)[None]
    spec_shape = jax.ShapeDtypeStruct((LAYERS, 1, KX, 2, CHAN, CHAN), F32)
    spec_scratch = (pltpu.VMEM((KX, 2, CHAN, CHAN), F32), pltpu.SemaphoreType.DMA)
    begun = local_call(
        early_kernel,
        "early_gradients",
        spec_shape,
        scalar_args=(0,),
        count=3,
        scratch=(pltpu.VMEM((16, 48, 128), F32),) + spec_scratch,
        far_outs=(0,),
    )(slot, early_near, early_far)
    spec_grad, mix_grad = local_call(
        gradient_kernel,
        "gradients",
        (spec_shape, jax.ShapeDtypeStruct((LAYERS, CHAN, CHAN), F32)),
        scalar_args=(0,),
        count=7,
        scratch=(pltpu.VMEM((16, 48, 128), F32), pltpu.VMEM((16, 32, 128), F32)) + spec_scratch,
        far_args=(1,),
        far_outs=(0,),
    )(slot, begun, early_near, early_far, held, other, lift)
    return advanced_displacement, advanced_fracture_state, spec_grad, mix_grad


def solution(mesh):
    return jax.shard_map(
        shards,
        mesh=mesh,
        in_specs=(
            P("grp", ("gx", "gy"), None),
            P("grp", ("gx", "gy"), None),
            P("grp", ("gx", "gy"), None),
            P("grp", ("gx", "gy"), None),
            P(),
            P(),
            P(),
            P(),
            P(("grp", "gy"), "gx", None),
            P(),
            P(),
            P(None, "gx", None, None, None, None),
            P(),
            P(),
            P(),
        ),
        out_specs=(
            P("grp", ("gx", "gy"), None),
            P("grp", ("gx", "gy"), None),
            P(None, "gx", None, None, None, None),
            P(),
        ),
        check_vma=False,
    )
```
